32 devices in a mesh: gx: 4 (over y, x), gy: 4 (over z), gz: 2 (over core).
Axes of the slice: x: 2, y: 2, z: 4, core: 2. Of those that a mesh axis runs over, the one named last changes fastest.
Arguments:
- potential: float32 [64, 64, 1024], P('gz', 'gx', 'gy'), may hold values from -4 to 4
- charge: float32 [64, 64, 1024], P('gz', 'gx', 'gy'), may hold values from -6 to 6
- permittivity: float32 [64, 64, 1024], P('gz', 'gx', 'gy'), may hold values from 2 to 80
- labels: int32 [64, 64, 1024], P('gz', 'gx', 'gy'), may hold values from 0 to 2
- pattern: int32 [16, 16, 4, 2], P('gz', 'gx', 'gy'), may hold values from 0 to 127
- blocks: float32 [16, 16, 4, 2, 64, 64], P('gz', 'gx', 'gy'), may hold values from -0.5 to 0.5
Outputs:
- potential_next: float32 [64, 64, 1024], P('gz', 'gx', 'gy')
- coarse_correction: float32 [16, 16, 4, 64], P('gz', 'gx', 'gy')
The draws below stay inside these ranges and needn't reach their ends.
All inputs are finite; a program needn't handle non-finite values.
Results may differ from the reference program's by a relative error of at most 0.00011.
Values sent between devices are 32-bit elements; how exact they have to be, the bound alone decides.
A program may use at most 64 MiB of HBM per device.

```python
import math
import jax
import jax.numpy as jnp
from jax import lax

AGG = 64
KB = 2
NZ = 64
NX = 64
NY = 1024
CZC = 8
NZC = 16
NXC = 16
NYA = 4
QCOL = 128


def with_ends(result, own_key, smallest, top_value):
    longest = result.shape.index(max(result.shape))
    spots = []
    for shift in (0, 1):
        where = [jax.random.randint(jax.random.fold_in(own_key, axis), (), 0, length) for axis, length in enumerate(result.shape)]
        where[longest] = (where[longest] + shift) % result.shape[longest]
        spots.append(tuple(where))
    return result.at[spots[0]].set(smallest).at[spots[1]].set(top_value)


def block_scale(rng, shape, split, low, high):
    level, own = 1.0, jax.random.fold_in(rng, 6)
    for position, shards_of in split:
        heights = jnp.exp(jax.random.uniform(jax.random.fold_in(own, position), (shards_of,), jnp.float32, low / len(split), high / len(split)))
        level = level * jnp.repeat(heights, shape[position] // shards_of).reshape([-1 if axis == position else 1 for axis in range(len(shape))])
    return level


def scatter_about(own_key, extent, scale, bound, split=(), dtype=jnp.bfloat16):
    values = scale * jax.random.normal(own_key, extent, jnp.float32)
    if split:
        values = values * block_scale(own_key, extent, split, -0.22, 0.18)
    return jnp.clip(values, -bound, bound).astype(dtype)


def setup_inputs(seed: int = 0) -> dict:
    key_of = jax.random.split(jax.random.key(seed), 7)
    potential = scatter_about(key_of[0], (NZ, NX, NY), 0.7, 4.0, ((0, 2), (1, 4), (2, 4)), jnp.float32)
    charge = scatter_about(key_of[1], (NZ, NX, NY), 1.0, 6.0, ((0, 2), (1, 4), (2, 4)), jnp.float32)
    permittivity = jnp.clip(jnp.exp(math.log(80.0) - 3.6888795 * jax.random.uniform(key_of[2], (NZ, NX, NY), jnp.float32) ** block_scale(key_of[2], (NZ, NX, NY), ((0, 2), (1, 4), (2, 4)), -0.2, 0.2)), 2.0, 80.0)
    labels = with_ends(jax.random.randint(key_of[3], (NZ, NX, NY), 0, 3), jax.random.fold_in(key_of[3], 1), 0, 2).astype(jnp.int32)
    pattern = with_ends(jax.random.randint(key_of[4], (NZC, NXC, NYA, KB), 0, QCOL), jax.random.fold_in(key_of[4], 1), 0, QCOL - 1).astype(jnp.int32)
    blocks = scatter_about(key_of[5], (NZC, NXC, NYA, KB, AGG, AGG), (AGG * KB) ** -0.5, 0.5, ((0, 2), (1, 4), (2, 4)), jnp.float32)
    return {"potential": potential, "charge": charge, "permittivity": permittivity, "labels": labels, "pattern": pattern, "blocks": blocks}


OMEGA = 0.8
CHARGE_SCALE = 40.0
COARSE_SCALE = 4.0


def screening_of(labels, permittivity):
    factor = jnp.where(labels == 1, 0.05, jnp.where(labels == 2, 0.2, 0.0))
    return factor * permittivity


def neighbours(padded):
    return (padded[2:, 1:-1, 1:-1], padded[:-2, 1:-1, 1:-1],
            padded[1:-1, 2:, 1:-1], padded[1:-1, :-2, 1:-1],
            padded[1:-1, 1:-1, 2:], padded[1:-1, 1:-1, :-2])


def stencil(pad_pot, pad_perm):
    centre_pot = pad_pot[1:-1, 1:-1, 1:-1]
    centre_perm = pad_perm[1:-1, 1:-1, 1:-1]
    net_flux = jnp.zeros_like(centre_pot)
    face_sum = jnp.zeros_like(centre_pot)
    for near_pot, near_perm in zip(neighbours(pad_pot), neighbours(pad_perm)):
        coupling = 0.5 * (centre_perm + near_perm)
        net_flux = net_flux + coupling * (centre_pot - near_pot)
        face_sum = face_sum + coupling
    return net_flux, face_sum


def reference(potential, charge, permittivity, labels, pattern, blocks):
    screening = screening_of(labels, permittivity)
    source = CHARGE_SCALE * charge
    pad_perm = jnp.pad(permittivity, 1)
    net_flux, face_sum = stencil(jnp.pad(potential, 1), pad_perm)
    diagonal = face_sum + screening * jnp.cosh(potential)
    swept = potential + OMEGA * (source - net_flux - screening * jnp.sinh(potential)) / diagonal
    swept_flux, unused = stencil(jnp.pad(swept, 1), pad_perm)
    residual = source - swept_flux - screening * jnp.sinh(swept)
    coarse_z = NZ // 4
    coarse_x = NX // 4
    y_aggs = NY // (4 * AGG)
    coarse_resid = residual.reshape(coarse_z, 4, coarse_x, 4, y_aggs, AGG, 4).sum(axis=(1, 3, 6)) / 64.0
    coarse_diag = diagonal.reshape(coarse_z, 4, coarse_x, 4, y_aggs, AGG, 4).sum(axis=(1, 3, 6)) / 64.0
    groups = coarse_z // CZC
    columns = coarse_resid.reshape(groups, CZC, coarse_x, y_aggs, AGG)
    columns = jnp.transpose(columns, (0, 3, 2, 1, 4)).reshape(groups, y_aggs, coarse_x * CZC, AGG)
    group_idx = (jnp.arange(coarse_z).astype(jnp.int32) // CZC)[:, None, None, None]
    yagg_idx = jnp.arange(y_aggs).astype(jnp.int32)[None, None, :, None]
    picked = columns[group_idx, yagg_idx, pattern.astype(jnp.int32)]
    coupled = jnp.einsum('zxjkab,zxjkb->zxja', blocks, picked, precision=lax.Precision.HIGHEST)
    correction = COARSE_SCALE * (coarse_resid + coupled) / coarse_diag
    spread = jnp.broadcast_to(correction[:, None, :, None, :, :, None],
                              (coarse_z, 4, coarse_x, 4, y_aggs, AGG, 4)).reshape(NZ, NX, NY)
    return swept + spread, correction
```

```python
import functools

import jax
import jax.numpy as jnp
from jax import lax
from jax.experimental import pallas as pl
from jax.experimental.pallas import tpu as pltpu
from jax.sharding import PartitionSpec as P

OMEGA = 0.8
CHARGE_SCALE = 40.0
COARSE_SCALE = 4.0
MESH = pl.DeviceIdType.MESH
F32 = jnp.float32
BF16 = jnp.bfloat16


def split2(value):
    high = value.astype(BF16)
    return high, (value - high.astype(F32)).astype(BF16)


def kernel(counts, Z, X, Y, A, pat, pot_h, chg_h, eps_h, lab_h, blk_h, out, corr,
           pot, chg, eps, lab, blk, num, dia, scr, wxs, wys, swp,
           zlo, zhi, xlo, xhi, ylo, yhi, xs_lo, xs_hi, ys,
           zlo2, zhi2, xlo2, xhi2, ylo2, yhi2, xs_lo2, xs_hi2, ys2,
           fx, zsr, zsd, weights, mine, col, picks, spread,
           in_sem, send_sem, recv_sem, gsend, grecv):
    ids = [lax.axis_index(name) for name in ("gx", "gy", "gz")]
    CZ, CX = Z // 4, X // 4
    NC = CZ * CX
    half = Y // 2

    loads = [pltpu.make_async_copy(s, d, in_sem.at[i])
             for i, (s, d) in enumerate(((pot_h, pot), (eps_h, eps), (chg_h, chg), (lab_h, lab), (blk_h, blk)))]
    for load in loads:
        load.start()

    def at(axis, index):
        return tuple(index if a == axis else ids[a] for a in range(3))

    def low_ok(axis):
        return ids[axis] > 0

    def high_ok(axis):
        return ids[axis] < counts[axis] - 1

    barrier = pltpu.get_barrier_semaphore()
    n = counts[0]
    for d in range(1, n):
        pl.semaphore_signal(barrier, inc=1, device_id=at(0, lax.rem(ids[0] + d, n)), device_id_type=MESH)
    expected = n - 1
    for axis in (1, 2):
        for ok, step in ((low_ok(axis), -1), (high_ok(axis), 1)):
            target = jnp.clip(ids[axis] + step, 0, counts[axis] - 1)

            @pl.when(ok)
            def _(target=target, axis=axis):
                pl.semaphore_signal(barrier, inc=1, device_id=at(axis, target), device_id_type=MESH)
            expected = expected + ok.astype(jnp.int32)

    for axis, lo_bufs, hi_bufs in ((2, (zlo, zlo2), (zhi, zhi2)), (0, (xlo, xlo2), (xhi, xhi2)), (1, (ylo, ylo2), (yhi, yhi2))):
        @pl.when(jnp.logical_not(low_ok(axis)))
        def _(bufs=lo_bufs):
            for b in bufs:
                b[...] = jnp.zeros_like(b)

        @pl.when(jnp.logical_not(high_ok(axis)))
        def _(bufs=hi_bufs):
            for b in bufs:
                b[...] = jnp.zeros_like(b)

    def up(axis, src, dst, sem):
        return (axis, True, pltpu.make_async_remote_copy(
            src_ref=src, dst_ref=dst, send_sem=send_sem.at[sem], recv_sem=recv_sem.at[sem],
            device_id=at(axis, jnp.minimum(ids[axis] + 1, counts[axis] - 1)), device_id_type=MESH))

    def down(axis, src, dst, sem):
        return (axis, False, pltpu.make_async_remote_copy(
            src_ref=src, dst_ref=dst, send_sem=send_sem.at[sem], recv_sem=recv_sem.at[sem],
            device_id=at(axis, jnp.maximum(ids[axis] - 1, 0)), device_id_type=MESH))

    def start(messages):
        for axis, upward, copy in messages:
            @pl.when(high_ok(axis) if upward else low_ok(axis))
            def _(copy=copy):
                copy.start()

    def wait_recv(messages):
        for axis, upward, copy in messages:
            @pl.when(low_ok(axis) if upward else high_ok(axis))
            def _(copy=copy):
                copy.wait_recv()

    def wait_send(messages):
        for axis, upward, copy in messages:
            @pl.when(high_ok(axis) if upward else low_ok(axis))
            def _(copy=copy):
                copy.wait_send()

    def slab(z):
        return pl.ds(pl.multiple_of(z * X, X), X)

    lane = lax.broadcasted_iota(jnp.int32, (X, 128), 1)
    pair = lane // 2
    row = lax.broadcasted_iota(jnp.int32, (X, Y), 0)
    ylane = lax.broadcasted_iota(jnp.int32, (X, Y), 1)

    def ends(value):
        return jnp.where(lane == 127, value[:, half:][:, -128:], value[:, :128])

    loads[0].wait()
    loads[1].wait()
    def pack1(z, acc):
        acc = jnp.where(pair == z, pltpu.roll(ends(pot[slab(z), :]), 2 * z + 1, 1), acc)
        return jnp.where(pair == z + 32, pltpu.roll(ends(eps[slab(z), :]), 2 * z + 65, 1), acc)
    ys[...] = lax.fori_loop(0, Z, pack1, jnp.zeros((X, 128), F32), unroll=8)
    for z in range(Z):
        for k, field in enumerate((pot, eps)):
            xs_lo[k * Z + z:k * Z + z + 1, :] = field[z * X:z * X + 1, :]
            xs_hi[k * Z + z:k * Z + z + 1, :] = field[z * X + X - 1:z * X + X, :]
    pl.semaphore_wait(barrier, expected)
    first = pl.ds(0, X)
    last = pl.ds((Z - 1) * X, X)
    halo1 = [
        up(0, xs_hi, xlo, 0), down(0, xs_lo, xhi, 1),
        up(1, ys, ylo, 2), down(1, ys, yhi, 3),
        up(2, pot.at[last, :], zlo.at[pl.ds(0, X), :], 4), up(2, eps.at[last, :], zlo.at[pl.ds(X, X), :], 5),
        down(2, pot.at[first, :], zhi.at[pl.ds(0, X), :], 6), down(2, eps.at[first, :], zhi.at[pl.ds(X, X), :], 7),
    ]
    start(halo1)
    loads[2].wait()
    loads[3].wait()

    not_top = row < X - 1
    not_end = ylane < Y - 1

    def sweep_local(z, carry):
        fz_prev, wz_prev = carry
        v, e = pot[slab(z), :], eps[slab(z), :]
        up_z = jnp.minimum(z + 1, Z - 1)
        inside = jnp.where(z < Z - 1, 0.5, 0.0).astype(F32)
        wz = inside * (e + eps[slab(up_z), :])
        fz = wz * (v - pot[slab(up_z), :])
        wx = jnp.where(not_top, 0.5 * (e + pltpu.roll(e, X - 1, 0)), 0.0)
        fxl = wx * (v - pltpu.roll(v, X - 1, 0))
        wy = jnp.where(not_end, 0.5 * (e + pltpu.roll(e, Y - 1, 1)), 0.0)
        fyl = wy * (v - pltpu.roll(v, Y - 1, 1))
        flux = (fz - fz_prev) + (fxl - pltpu.roll(fxl, 1, 0)) + (fyl - pltpu.roll(fyl, 1, 1))
        faces = (wz + wz_prev) + (wx + pltpu.roll(wx, 1, 0)) + (wy + pltpu.roll(wy, 1, 1))
        labels = lab[slab(z), :]
        s = e * jnp.where(labels == 1, 0.05, jnp.where(labels == 2, 0.2, 0.0))
        ep, em = jnp.exp(v), jnp.exp(-v)
        wxs[slab(z), :] = wx
        wys[slab(z), :] = wy
        scr[slab(z), :] = s
        num[slab(z), :] = CHARGE_SCALE * chg[slab(z), :] - flux - s * (0.5 * (ep - em))
        dia[slab(z), :] = faces + s * (0.5 * (ep + em))
        return fz, wz
    zero = jnp.zeros((X, Y), F32)
    lax.fori_loop(0, Z, sweep_local, (zero, zero), unroll=2)

    wait_recv(halo1)
    wz_lo = 0.5 * (eps[first, :] + zlo[X:2 * X, :])
    wz_hi = 0.5 * (eps[last, :] + zhi[X:2 * X, :])
    num[first, :] = num[first, :] - wz_lo * (pot[first, :] - zlo[0:X, :])
    num[last, :] = num[last, :] - wz_hi * (pot[last, :] - zhi[0:X, :])
    dia[first, :] = dia[first, :] + wz_lo
    dia[last, :] = dia[last, :] + wz_hi
    for k, (own, halo) in enumerate(((xs_lo, xlo), (xs_hi, xhi))):
        w = 0.5 * (own[Z:2 * Z, :] + halo[Z:2 * Z, :])
        fx[2 * k * Z:(2 * k + 1) * Z, :] = w * (own[0:Z, :] - halo[0:Z, :])
        fx[(2 * k + 1) * Z:(2 * k + 2) * Z, :] = w
    even = lane % 2 == 0
    own_y = pltpu.roll(ys[...], 127, 1)
    halo_y = jnp.where(even, ylo[...], pltpu.roll(yhi[...], 126, 1))
    wy_end = 0.5 * (pltpu.roll(own_y, 64, 1) + pltpu.roll(halo_y, 64, 1))
    fy_end = wy_end * (own_y - halo_y)

    def at_ends(value):
        return jnp.concatenate([jnp.where(lane == 0, value, 0.0), jnp.where(lane == 127, value, 0.0)], axis=1)

    def sweep(zc, acc):
        total = jnp.zeros((X, Y), F32)
        for dz in range(4):
            z = zc * 4 + dz
            shift = lax.rem(128 - 2 * z, 128)
            f = at_ends(pltpu.roll(fy_end, shift, 1))
            w = at_ends(pltpu.roll(wy_end, shift, 1))
            f = f + jnp.where(row == 0, fx[pl.ds(z, 1), :], 0.0) + jnp.where(row == X - 1, fx[pl.ds(2 * Z + z, 1), :], 0.0)
            w = w + jnp.where(row == 0, fx[pl.ds(Z + z, 1), :], 0.0) + jnp.where(row == X - 1, fx[pl.ds(3 * Z + z, 1), :], 0.0)
            d = dia[slab(z), :] + w
            total = total + d
            sw = pot[slab(z), :] + OMEGA * (num[slab(z), :] - f) / d
            swp[slab(z), :] = sw
            xs_lo2[pl.ds(z, 1), :] = sw[0:1, :]
            xs_hi2[pl.ds(z, 1), :] = sw[X - 1:X, :]
            acc = jnp.where(pair == z, pltpu.roll(ends(sw), 2 * z + 1, 1), acc)
        zsd[slab(zc), :] = total
        return acc
    ys2[...] = lax.fori_loop(0, CZ, sweep, jnp.zeros((X, 128), F32))

    halo2 = [
        up(0, xs_hi2, xlo2, 8), down(0, xs_lo2, xhi2, 9),
        up(1, ys2, ylo2, 10), down(1, ys2, yhi2, 11),
        up(2, swp.at[last, :], zlo2, 12), down(2, swp.at[first, :], zhi2, 13),
    ]
    start(halo2)

    def residual_local(zc, fz_prev):
        total = jnp.zeros((X, Y), F32)
        for dz in range(4):
            z = zc * 4 + dz
            v, e = swp[slab(z), :], eps[slab(z), :]
            up_z = jnp.minimum(z + 1, Z - 1)
            inside = jnp.where(z < Z - 1, 0.5, 0.0).astype(F32)
            fz = inside * (e + eps[slab(up_z), :]) * (v - swp[slab(up_z), :])
            fxl = wxs[slab(z), :] * (v - pltpu.roll(v, X - 1, 0))
            fyl = wys[slab(z), :] * (v - pltpu.roll(v, Y - 1, 1))
            flux = (fz - fz_prev) + (fxl - pltpu.roll(fxl, 1, 0)) + (fyl - pltpu.roll(fyl, 1, 1))
            total = total + (CHARGE_SCALE * chg[slab(z), :] - flux - scr[slab(z), :] * (0.5 * (jnp.exp(v) - jnp.exp(-v))))
            fz_prev = fz
        zsr[slab(zc), :] = total
        return fz_prev
    lax.fori_loop(0, CZ, residual_local, zero)

    loads[4].wait()
    def split_blocks(zc, c):
        for xc in range(CX):
            at_block = (zc * CX + xc) * 2
            both = jnp.concatenate([blk[at_block], blk[at_block + 1]], axis=1)
            high, low = split2(both)
            weights[zc, xc * A:(xc + 1) * A, 0:2 * A] = high
            weights[zc, xc * A:(xc + 1) * A, 2 * A:4 * A] = low
        return c
    lax.fori_loop(0, CZ, split_blocks, 0)

    merge = jnp.where(lax.broadcasted_iota(jnp.int32, (Y, 128), 0) // 4 == lax.broadcasted_iota(jnp.int32, (Y, 128), 1) % A, 1.0, 0.0).astype(BF16)

    def coarse_rows(ref):
        groups = []
        for xc in range(CX):
            rows = []
            for zc in range(CZ):
                base = zc * X + 4 * xc
                block = ref[zc * X + (xc // 2) * 8:zc * X + (xc // 2) * 8 + 8, :]
                rows.append(jnp.sum(block[(xc % 2) * 4:(xc % 2) * 4 + 4, :], axis=0, keepdims=True))
            groups.append(jnp.concatenate(rows, axis=0))
        return groups

    def merged(groups):
        high, low = split2(jnp.concatenate(groups, axis=0))
        both = jnp.dot(jnp.concatenate([high, low], axis=0), merge, preferred_element_type=F32)
        return (both[0:NC, :] + both[NC:2 * NC, :]) * (1.0 / 64.0)

    coarse_diag = merged(coarse_rows(zsd))

    wait_recv(halo2)
    zsr[0:X, :] = zsr[0:X, :] - wz_lo * (swp[first, :] - zlo2[...])
    zsr[(CZ - 1) * X:CZ * X, :] = zsr[(CZ - 1) * X:CZ * X, :] - wz_hi * (swp[last, :] - zhi2[...])
    own_y = pltpu.roll(ys2[...], 127, 1)
    halo_y = jnp.where(even, ylo2[...], pltpu.roll(yhi2[...], 126, 1))
    f = wy_end * (own_y - halo_y)
    f = f + pltpu.roll(f, 126, 1)
    f = f + pltpu.roll(f, 124, 1)
    for zc in range(CZ):
        zsr[zc * X:(zc + 1) * X, :] = zsr[zc * X:(zc + 1) * X, :] - at_ends(pltpu.roll(f, (128 - 8 * zc) % 128, 1))
    groups = coarse_rows(zsr)
    for k, (own, halo, xc) in enumerate(((xs_lo2, xlo2, 0), (xs_hi2, xhi2, CX - 1))):
        f = fx[(2 * k + 1) * Z:(2 * k + 2) * Z, :] * (own[...] - halo[...])
        groups[xc] = groups[xc] - jnp.concatenate(
            [jnp.sum(f[4 * zc:4 * zc + 4, :], axis=0, keepdims=True) for zc in range(CZ)], axis=0)
    coarse_resid = merged(groups)
    mine[...] = coarse_resid
    my_rows = pl.ds(pl.multiple_of(ids[0] * NC, NC), NC)
    gathers = []
    for d in range(1, n):
        copy = pltpu.make_async_remote_copy(
            src_ref=mine, dst_ref=col.at[my_rows, :], send_sem=gsend.at[d - 1], recv_sem=grecv.at[d - 1],
            device_id=at(0, lax.rem(ids[0] + d, n)), device_id_type=MESH)
        copy.start()
        gathers.append(copy)
    col[my_rows, :] = coarse_resid
    for copy in gathers:
        copy.wait_recv()

    left = lax.broadcasted_iota(jnp.int32, (1, 128), 1) < A
    for zc in range(CZ):
        for xc in range(CX):
            p = jnp.where(left, col[pl.ds(pat[zc, xc, 0, 0], 1), :], col[pl.ds(pat[zc, xc, 0, 1], 1), :])
            picks[zc * 8 + xc:zc * 8 + xc + 1, :] = p
            picks[zc * 8 + 4 + xc:zc * 8 + 5 + xc, :] = p
    half_row = lax.broadcasted_iota(jnp.int32, (8, 128), 0) < 4
    own_block = (lax.broadcasted_iota(jnp.int32, (8, 4 * A), 0) % 4) == (lax.broadcasted_iota(jnp.int32, (8, 4 * A), 1) // A)
    rows = []
    for zc in range(CZ):
        p = picks[zc * 8:zc * 8 + 8, :]
        high = p.astype(BF16).astype(F32)
        lhs = jnp.concatenate([jnp.where(half_row, high, p - high), jnp.where(half_row, high, 0.0)], axis=1).astype(BF16)
        prod = lax.dot_general(lhs, weights[zc], (((1,), (1,)), ((), ())), preferred_element_type=F32)
        rows.append(jnp.sum(jnp.where(own_block, prod, 0.0), axis=0, keepdims=True))
    coupled = jnp.concatenate(rows, axis=0)

    def by_lane(value):
        parts = [value[xc * CZ:(xc + 1) * CZ, :] for xc in range(CX)]
        return jnp.concatenate([jnp.where(left, parts[i], parts[i + 1]) for i in range(0, CX, 2)], axis=1)

    correction = COARSE_SCALE * (by_lane(coarse_resid) + coupled) / by_lane(coarse_diag)
    for xc in range(CX):
        corr[:, xc, 0, :] = correction[:, xc * A:(xc + 1) * A]
    stacked = []
    for xc in range(CX):
        part = correction[:, (xc // 2) * 128:(xc // 2) * 128 + 128]
        stacked.append(jnp.where(left if xc % 2 == 0 else jnp.logical_not(left), part, 0.0))
    high, low = split2(jnp.concatenate(stacked, axis=0))
    both = lax.dot_general(jnp.concatenate([high, low], axis=0), merge, (((1,), (1,)), ((), ())), preferred_element_type=F32)
    spread[...] = both[0:NC, :] + both[NC:2 * NC, :]
    quarter = row // 4

    def finish(zc, c):
        add = jnp.zeros((X, Y), F32)
        for xc in range(CX):
            add = jnp.where(quarter == xc, spread[pl.ds(xc * CZ + zc, 1), :], add)
        for dz in range(4):
            z = zc * 4 + dz
            out[slab(z), :] = swp[slab(z), :] + add
        return c
    lax.fori_loop(0, CZ, finish, 0)

    wait_send(halo1)
    wait_send(halo2)
    for copy in gathers:
        copy.wait_send()


def solution(mesh):
    counts = (mesh.shape["gx"], mesh.shape["gy"], mesh.shape["gz"])

    def per_device(potential, charge, permittivity, labels, pattern, blocks):
        Z, X, Y = potential.shape
        A = blocks.shape[-1]
        CZ, CX = Z // 4, X // 4
        NC = CZ * CX
        flat = (Z * X, Y)
        whole = pltpu.VMEM(flat, F32)
        any_spec = pl.BlockSpec(memory_space=pl.ANY)
        vmem = pl.BlockSpec(memory_space=pltpu.VMEM)
        n = counts[0]

        def halo_scratch(k):
            return [pltpu.VMEM((k * X, Y), F32)] * 2 + [pltpu.VMEM((k * Z, Y), F32)] * 2 + [pltpu.VMEM((X, 128), F32)] * 2 + \
                [pltpu.VMEM((k * Z, Y), F32)] * 2 + [pltpu.VMEM((X, 128), F32)]

        out, corr = pl.pallas_call(
            functools.partial(kernel, counts, Z, X, Y, A),
            out_shape=(jax.ShapeDtypeStruct(flat, F32), jax.ShapeDtypeStruct((CZ, CX, 1, A), F32)),
            in_specs=[pl.BlockSpec(memory_space=pltpu.SMEM)] + [any_spec] * 5,
            out_specs=(vmem, vmem),
            scratch_shapes=[
                whole, whole, whole, pltpu.VMEM(flat, jnp.int32), pltpu.VMEM((2 * NC, A, A), F32),
                whole, whole, whole, whole, whole, whole,
                *halo_scratch(2), *halo_scratch(1),
                pltpu.VMEM((4 * Z, Y), F32), pltpu.VMEM((CZ * X, Y), F32), pltpu.VMEM((CZ * X, Y), F32),
                pltpu.VMEM((CZ, CX * A, 4 * A), BF16), pltpu.VMEM((NC, 128), F32), pltpu.VMEM((n * NC, 128), F32),
                pltpu.VMEM((8 * CZ, 128), F32), pltpu.VMEM((NC, Y), F32),
                pltpu.SemaphoreType.DMA((5,)), pltpu.SemaphoreType.DMA((14,)), pltpu.SemaphoreType.DMA((14,)),
                pltpu.SemaphoreType.DMA((n,)), pltpu.SemaphoreType.DMA((n,)),
            ],
            compiler_params=pltpu.CompilerParams(
                collective_id=0, has_side_effects=True, vmem_limit_bytes=32 * 1024 * 1024),
        )(pattern, potential.reshape(flat), charge.reshape(flat), permittivity.reshape(flat), labels.reshape(flat),
          blocks.reshape(2 * NC, A, A))
        return out.reshape(Z, X, Y), corr

    return jax.shard_map(
        per_device,
        mesh=mesh,
        in_specs=(
            P("gz", "gx", "gy"),
            P("gz", "gx", "gy"),
            P("gz", "gx", "gy"),
            P("gz", "gx", "gy"),
            P("gz", "gx", "gy", None),
            P("gz", "gx", "gy", None, None, None),
        ),
        out_specs=(P("gz", "gx", "gy"), P("gz", "gx", "gy", None)),
        check_vma=False,
    )
```

```python
import functools

import jax
import jax.numpy as jnp
from jax import lax
from jax.experimental import pallas as pl
from jax.experimental.pallas import tpu as pltpu
from jax.sharding import PartitionSpec as P

OMEGA = 0.8
CHARGE_SCALE = 40.0
COARSE_SCALE = 4.0
MESH = pl.DeviceIdType.MESH
F32 = jnp.float32
BF16 = jnp.bfloat16


def split2(value):
    high = value.astype(BF16)
    return high, (value - high.astype(F32)).astype(BF16)


def kernel(counts, Z, X, Y, A, pat_h, pot_h, chg_h, eps_h, lab_h, blk_h, out, corr,
           pat, pot, chg, eps, lab, blk, num, dia, scr, wxs, wys, swp,
           zlo, zhi, xlo, xhi, ylo, yhi, xs_lo, xs_hi, ys,
           zlo2, zhi2, xlo2, xhi2, ylo2, yhi2, xs_lo2, xs_hi2, ys2,
           fx, zsr, zsd, weights, mine, col, choose, spread,
           in_sem, send_sem, recv_sem, gsend, grecv):
    ids = [lax.axis_index(name) for name in ("gx", "gy", "gz")]
    CZ, CX = Z // 4, X // 4
    NC = CZ * CX
    half = Y // 2

    loads = [pltpu.make_async_copy(s, d, in_sem.at[i])
             for i, (s, d) in enumerate(((pot_h, pot), (eps_h, eps), (chg_h, chg), (lab_h, lab), (pat_h, pat), (blk_h, blk)))]
    for load in loads[:5]:
        load.start()

    def at(axis, index):
        return tuple(index if a == axis else ids[a] for a in range(3))

    def low_ok(axis):
        return ids[axis] > 0

    def high_ok(axis):
        return ids[axis] < counts[axis] - 1

    barrier = pltpu.get_barrier_semaphore()
    n = counts[0]
    for d in range(1, n):
        pl.semaphore_signal(barrier, inc=1, device_id=at(0, lax.rem(ids[0] + d, n)), device_id_type=MESH)
    expected = n - 1
    for axis in (1, 2):
        for ok, step in ((low_ok(axis), -1), (high_ok(axis), 1)):
            target = jnp.clip(ids[axis] + step, 0, counts[axis] - 1)

            @pl.when(ok)
            def _(target=target, axis=axis):
                pl.semaphore_signal(barrier, inc=1, device_id=at(axis, target), device_id_type=MESH)
            expected = expected + ok.astype(jnp.int32)

    for axis, lo_bufs, hi_bufs in ((2, (zlo, zlo2), (zhi, zhi2)), (0, (xlo, xlo2), (xhi, xhi2)), (1, (ylo, ylo2), (yhi, yhi2))):
        @pl.when(jnp.logical_not(low_ok(axis)))
        def _(bufs=lo_bufs):
            for b in bufs:
                b[...] = jnp.zeros_like(b)

        @pl.when(jnp.logical_not(high_ok(axis)))
        def _(bufs=hi_bufs):
            for b in bufs:
                b[...] = jnp.zeros_like(b)

    def up(axis, src, dst, sem):
        return (axis, True, pltpu.make_async_remote_copy(
            src_ref=src, dst_ref=dst, send_sem=send_sem.at[sem], recv_sem=recv_sem.at[sem],
            device_id=at(axis, jnp.minimum(ids[axis] + 1, counts[axis] - 1)), device_id_type=MESH))

    def down(axis, src, dst, sem):
        return (axis, False, pltpu.make_async_remote_copy(
            src_ref=src, dst_ref=dst, send_sem=send_sem.at[sem], recv_sem=recv_sem.at[sem],
            device_id=at(axis, jnp.maximum(ids[axis] - 1, 0)), device_id_type=MESH))

    def start(messages):
        for axis, upward, copy in messages:
            @pl.when(high_ok(axis) if upward else low_ok(axis))
            def _(copy=copy):
                copy.start()

    def wait_recv(messages):
        for axis, upward, copy in messages:
            @pl.when(low_ok(axis) if upward else high_ok(axis))
            def _(copy=copy):
                copy.wait_recv()

    def wait_send(messages):
        for axis, upward, copy in messages:
            @pl.when(high_ok(axis) if upward else low_ok(axis))
            def _(copy=copy):
                copy.wait_send()

    def slab(z):
        return pl.ds(pl.multiple_of(z * X, X), X)

    lane = lax.broadcasted_iota(jnp.int32, (X, 128), 1)
    pair = lane // 2
    row = lax.broadcasted_iota(jnp.int32, (X, Y), 0)
    ylane = lax.broadcasted_iota(jnp.int32, (X, Y), 1)

    def ends(value):
        return jnp.where(lane == 127, value[:, half:][:, -128:], value[:, :128])

    loads[0].wait()
    loads[1].wait()
    loads[5].start()
    def pack1(z, acc):
        acc = jnp.where(pair == z, pltpu.roll(ends(pot[slab(z), :]), 2 * z + 1, 1), acc)
        return jnp.where(pair == z + 32, pltpu.roll(ends(eps[slab(z), :]), 2 * z + 65, 1), acc)
    ys[...] = lax.fori_loop(0, Z, pack1, jnp.zeros((X, 128), F32), unroll=8)
    for z in range(Z):
        for k, field in enumerate((pot, eps)):
            xs_lo[k * Z + z:k * Z + z + 1, :] = field[z * X:z * X + 1, :]
            xs_hi[k * Z + z:k * Z + z + 1, :] = field[z * X + X - 1:z * X + X, :]
    pl.semaphore_wait(barrier, expected)
    first = pl.ds(0, X)
    last = pl.ds((Z - 1) * X, X)
    halo1 = [
        up(0, xs_hi, xlo, 0), down(0, xs_lo, xhi, 1),
        up(1, ys, ylo, 2), down(1, ys, yhi, 3),
        up(2, pot.at[last, :], zlo.at[pl.ds(0, X), :], 4), up(2, eps.at[last, :], zlo.at[pl.ds(X, X), :], 5),
        down(2, pot.at[first, :], zhi.at[pl.ds(0, X), :], 6), down(2, eps.at[first, :], zhi.at[pl.ds(X, X), :], 7),
    ]
    start(halo1)
    loads[2].wait()
    loads[3].wait()

    not_top = row < X - 1
    not_end = ylane < Y - 1

    def sweep_local(z, carry):
        fz_prev, wz_prev = carry
        v, e = pot[slab(z), :], eps[slab(z), :]
        up_z = jnp.minimum(z + 1, Z - 1)
        inside = jnp.where(z < Z - 1, 0.5, 0.0).astype(F32)
        wz = inside * (e + eps[slab(up_z), :])
        fz = wz * (v - pot[slab(up_z), :])
        wx = jnp.where(not_top, 0.5 * (e + pltpu.roll(e, X - 1, 0)), 0.0)
        fxl = wx * (v - pltpu.roll(v, X - 1, 0))
        wy = jnp.where(not_end, 0.5 * (e + pltpu.roll(e, Y - 1, 1)), 0.0)
        fyl = wy * (v - pltpu.roll(v, Y - 1, 1))
        flux = (fz - fz_prev) + (fxl - pltpu.roll(fxl, 1, 0)) + (fyl - pltpu.roll(fyl, 1, 1))
        faces = (wz + wz_prev) + (wx + pltpu.roll(wx, 1, 0)) + (wy + pltpu.roll(wy, 1, 1))
        labels = lab[slab(z), :]
        s = e * jnp.where(labels == 1, 0.05, jnp.where(labels == 2, 0.2, 0.0))
        ep, em = jnp.exp(v), jnp.exp(-v)
        wxs[slab(z), :] = wx
        wys[slab(z), :] = wy
        scr[slab(z), :] = s
        num[slab(z), :] = CHARGE_SCALE * chg[slab(z), :] - flux - s * (0.5 * (ep - em))
        dia[slab(z), :] = faces + s * (0.5 * (ep + em))
        return fz, wz
    zero = jnp.zeros((X, Y), F32)
    lax.fori_loop(0, Z, sweep_local, (zero, zero), unroll=2)

    wait_recv(halo1)
    wz_lo = 0.5 * (eps[first, :] + zlo[X:2 * X, :])
    wz_hi = 0.5 * (eps[last, :] + zhi[X:2 * X, :])
    num[first, :] = num[first, :] - wz_lo * (pot[first, :] - zlo[0:X, :])
    num[last, :] = num[last, :] - wz_hi * (pot[last, :] - zhi[0:X, :])
    dia[first, :] = dia[first, :] + wz_lo
    dia[last, :] = dia[last, :] + wz_hi
    for k, (own, halo) in enumerate(((xs_lo, xlo), (xs_hi, xhi))):
        w = 0.5 * (own[Z:2 * Z, :] + halo[Z:2 * Z, :])
        fx[2 * k * Z:(2 * k + 1) * Z, :] = w * (own[0:Z, :] - halo[0:Z, :])
        fx[(2 * k + 1) * Z:(2 * k + 2) * Z, :] = w
    even = lane % 2 == 0
    own_y = pltpu.roll(ys[...], 127, 1)
    halo_y = jnp.where(even, ylo[...], pltpu.roll(yhi[...], 126, 1))
    wy_end = 0.5 * (pltpu.roll(own_y, 64, 1) + pltpu.roll(halo_y, 64, 1))
    fy_end = wy_end * (own_y - halo_y)

    def at_ends(value):
        return jnp.concatenate([jnp.where(lane == 0, value, 0.0), jnp.where(lane == 127, value, 0.0)], axis=1)

    def sweep(zc, acc):
        total = jnp.zeros((X, Y), F32)
        for dz in range(4):
            z = zc * 4 + dz
            shift = lax.rem(128 - 2 * z, 128)
            f = at_ends(pltpu.roll(fy_end, shift, 1))
            w = at_ends(pltpu.roll(wy_end, shift, 1))
            f = f + jnp.where(row == 0, fx[pl.ds(z, 1), :], 0.0) + jnp.where(row == X - 1, fx[pl.ds(2 * Z + z, 1), :], 0.0)
            w = w + jnp.where(row == 0, fx[pl.ds(Z + z, 1), :], 0.0) + jnp.where(row == X - 1, fx[pl.ds(3 * Z + z, 1), :], 0.0)
            d = dia[slab(z), :] + w
            total = total + d
            sw = pot[slab(z), :] + OMEGA * (num[slab(z), :] - f) / d
            swp[slab(z), :] = sw
            xs_lo2[pl.ds(z, 1), :] = sw[0:1, :]
            xs_hi2[pl.ds(z, 1), :] = sw[X - 1:X, :]
            acc = jnp.where(pair == z, pltpu.roll(ends(sw), 2 * z + 1, 1), acc)
        zsd[slab(zc), :] = total
        return acc
    ys2[...] = lax.fori_loop(0, CZ, sweep, jnp.zeros((X, 128), F32))

    halo2 = [
        up(0, xs_hi2, xlo2, 8), down(0, xs_lo2, xhi2, 9),
        up(1, ys2, ylo2, 10), down(1, ys2, yhi2, 11),
        up(2, swp.at[last, :], zlo2, 12), down(2, swp.at[first, :], zhi2, 13),
    ]
    start(halo2)

    def residual_local(zc, fz_prev):
        total = jnp.zeros((X, Y), F32)
        for dz in range(4):
            z = zc * 4 + dz
            v, e = swp[slab(z), :], eps[slab(z), :]
            up_z = jnp.minimum(z + 1, Z - 1)
            inside = jnp.where(z < Z - 1, 0.5, 0.0).astype(F32)
            fz = inside * (e + eps[slab(up_z), :]) * (v - swp[slab(up_z), :])
            fxl = wxs[slab(z), :] * (v - pltpu.roll(v, X - 1, 0))
            fyl = wys[slab(z), :] * (v - pltpu.roll(v, Y - 1, 1))
            flux = (fz - fz_prev) + (fxl - pltpu.roll(fxl, 1, 0)) + (fyl - pltpu.roll(fyl, 1, 1))
            total = total + (CHARGE_SCALE * chg[slab(z), :] - flux - scr[slab(z), :] * (0.5 * (jnp.exp(v) - jnp.exp(-v))))
            fz_prev = fz
        zsr[slab(zc), :] = total
        return fz_prev
    lax.fori_loop(0, CZ, residual_local, zero)

    loads[5].wait()
    def split_blocks(zc, c):
        for xc in range(CX):
            at_block = (zc * CX + xc) * 2
            both = jnp.concatenate([blk[at_block], blk[at_block + 1]], axis=1)
            high, low = split2(both)
            here = pl.ds(pl.multiple_of(zc * A, A), A)
            weights[xc, here, 0:2 * A] = high
            weights[xc, here, 2 * A:4 * A] = low
        return c
    lax.fori_loop(0, CZ, split_blocks, 0)

    loads[4].wait()
    diagonal = lax.broadcasted_iota(jnp.int32, (CZ, CZ), 0) == lax.broadcasted_iota(jnp.int32, (CZ, CZ), 1)
    names = lax.broadcasted_iota(jnp.int32, (CZ, n * NC), 1).astype(F32)
    for k in range(2):
        for xc in range(CX):
            wanted = jnp.sum(jnp.where(diagonal, pat[xc, 0, k:k + 1, :].astype(F32), 0.0), axis=1, keepdims=True)
            at_row = (k * CX + xc) * CZ
            choose[at_row:at_row + CZ, :] = jnp.where(names == wanted, 1.0, 0.0)

    merge = jnp.where(lax.broadcasted_iota(jnp.int32, (Y, 128), 0) // 4 == lax.broadcasted_iota(jnp.int32, (Y, 128), 1) % A, 1.0, 0.0).astype(BF16)

    def coarse_rows(ref):
        groups = []
        for xc in range(CX):
            rows = []
            for zc in range(CZ):
                base = zc * X + 4 * xc
                block = ref[zc * X + (xc // 2) * 8:zc * X + (xc // 2) * 8 + 8, :]
                rows.append(jnp.sum(block[(xc % 2) * 4:(xc % 2) * 4 + 4, :], axis=0, keepdims=True))
            groups.append(jnp.concatenate(rows, axis=0))
        return groups

    def merged(groups):
        high, low = split2(jnp.concatenate(groups, axis=0))
        both = jnp.dot(jnp.concatenate([high, low], axis=0), merge, preferred_element_type=F32)
        return (both[0:NC, :] + both[NC:2 * NC, :]) * (1.0 / 64.0)

    coarse_diag = merged(coarse_rows(zsd))

    wait_recv(halo2)
    zsr[0:X, :] = zsr[0:X, :] - wz_lo * (swp[first, :] - zlo2[...])
    zsr[(CZ - 1) * X:CZ * X, :] = zsr[(CZ - 1) * X:CZ * X, :] - wz_hi * (swp[last, :] - zhi2[...])
    own_y = pltpu.roll(ys2[...], 127, 1)
    halo_y = jnp.where(even, ylo2[...], pltpu.roll(yhi2[...], 126, 1))
    f = wy_end * (own_y - halo_y)
    f = f + pltpu.roll(f, 126, 1)
    f = f + pltpu.roll(f, 124, 1)
    for zc in range(CZ):
        zsr[zc * X:(zc + 1) * X, :] = zsr[zc * X:(zc + 1) * X, :] - at_ends(pltpu.roll(f, (128 - 8 * zc) % 128, 1))
    groups = coarse_rows(zsr)
    for k, (own, halo, xc) in enumerate(((xs_lo2, xlo2, 0), (xs_hi2, xhi2, CX - 1))):
        f = fx[(2 * k + 1) * Z:(2 * k + 2) * Z, :] * (own[...] - halo[...])
        groups[xc] = groups[xc] - jnp.concatenate(
            [jnp.sum(f[4 * zc:4 * zc + 4, :], axis=0, keepdims=True) for zc in range(CZ)], axis=0)
    coarse_resid = merged(groups)
    mine[...] = coarse_resid
    my_rows = pl.ds(pl.multiple_of(ids[0] * NC, NC), NC)
    gathers = []
    for d in range(1, n):
        copy = pltpu.make_async_remote_copy(
            src_ref=mine, dst_ref=col.at[my_rows, :], send_sem=gsend.at[d - 1], recv_sem=grecv.at[d - 1],
            device_id=at(0, lax.rem(ids[0] + d, n)), device_id_type=MESH)
        copy.start()
        gathers.append(copy)
    col[my_rows, :] = coarse_resid
    for copy in gathers:
        copy.wait_recv()

    left = lax.broadcasted_iota(jnp.int32, (CZ, 128), 1) < A
    picked = jnp.dot(choose[...].astype(BF16), jnp.concatenate(split2(col[...]), axis=1), preferred_element_type=F32)
    zrow = lax.broadcasted_iota(jnp.int32, (CZ, 128), 0)
    rows = []
    for xc in range(CX):
        p0, p1 = picked[xc * CZ:(xc + 1) * CZ, :], picked[(CX + xc) * CZ:(CX + xc + 1) * CZ, :]
        high, low = [jnp.where(left, p0[:, i:i + 128], p1[:, i:i + 128]) for i in (0, 128)]
        lhs = jnp.concatenate([jnp.concatenate([high, high], axis=1),
                               jnp.concatenate([low, jnp.zeros_like(low)], axis=1)], axis=0).astype(BF16)
        prod = lax.dot_general(lhs, weights[xc], (((1,), (1,)), ((), ())), preferred_element_type=F32)
        prod = prod[0:CZ, :] + prod[CZ:2 * CZ, :]
        mine_only = jnp.zeros((CZ, 128), F32)
        for i in range(CZ // 2):
            mine_only = jnp.where(zrow // 2 == i, prod[:, i * 128:(i + 1) * 128], mine_only)
        rows.append(jnp.where(left == (zrow % 2 == 0), mine_only, pltpu.roll(mine_only, A, 1)))
    coupled = jnp.concatenate(rows, axis=0)

    correction = COARSE_SCALE * (coarse_resid + coupled) / coarse_diag
    for xc in range(CX):
        corr[:, xc, 0, :] = correction[xc * CZ:(xc + 1) * CZ, 0:A]
    high, low = split2(jnp.where(lax.broadcasted_iota(jnp.int32, (NC, 128), 1) < A, correction, 0.0))
    both = lax.dot_general(jnp.concatenate([high, low], axis=0), merge, (((1,), (1,)), ((), ())), preferred_element_type=F32)
    spread[...] = both[0:NC, :] + both[NC:2 * NC, :]
    quarter = row // 4

    def finish(zc, c):
        add = jnp.zeros((X, Y), F32)
        for xc in range(CX):
            add = jnp.where(quarter == xc, spread[pl.ds(xc * CZ + zc, 1), :], add)
        for dz in range(4):
            z = zc * 4 + dz
            out[slab(z), :] = swp[slab(z), :] + add
        return c
    lax.fori_loop(0, CZ, finish, 0)

    wait_send(halo1)
    wait_send(halo2)
    for copy in gathers:
        copy.wait_send()


def solution(mesh):
    counts = (mesh.shape["gx"], mesh.shape["gy"], mesh.shape["gz"])

    def per_device(potential, charge, permittivity, labels, pattern, blocks):
        Z, X, Y = potential.shape
        A = blocks.shape[-1]
        CZ, CX = Z // 4, X // 4
        NC = CZ * CX
        flat = (Z * X, Y)
        whole = pltpu.VMEM(flat, F32)
        any_spec = pl.BlockSpec(memory_space=pltpu.HBM)
        vmem = pl.BlockSpec(memory_space=pltpu.VMEM)
        n = counts[0]

        def halo_scratch(k):
            return [pltpu.VMEM((k * X, Y), F32)] * 2 + [pltpu.VMEM((k * Z, Y), F32)] * 2 + [pltpu.VMEM((X, 128), F32)] * 2 + \
                [pltpu.VMEM((k * Z, Y), F32)] * 2 + [pltpu.VMEM((X, 128), F32)]

        out, corr = pl.pallas_call(
            functools.partial(kernel, counts, Z, X, Y, A),
            out_shape=(jax.ShapeDtypeStruct(flat, F32), jax.ShapeDtypeStruct((CZ, CX, 1, A), F32)),
            in_specs=[any_spec] * 6,
            out_specs=(vmem, vmem),
            scratch_shapes=[
                pltpu.VMEM((CX, 1, 2, CZ), jnp.int32), whole, whole, whole, pltpu.VMEM(flat, jnp.int32), pltpu.VMEM((2 * NC, A, A), F32),
                whole, whole, whole, whole, whole, whole,
                *halo_scratch(2), *halo_scratch(1),
                pltpu.VMEM((4 * Z, Y), F32), pltpu.VMEM((CZ * X, Y), F32), pltpu.VMEM((CZ * X, Y), F32),
                pltpu.VMEM((CX, CZ * A, 4 * A), BF16), pltpu.VMEM((NC, 128), F32), pltpu.VMEM((n * NC, 128), F32),
                pltpu.VMEM((2 * NC, n * NC), F32), pltpu.VMEM((NC, Y), F32),
                pltpu.SemaphoreType.DMA((6,)), pltpu.SemaphoreType.DMA((14,)), pltpu.SemaphoreType.DMA((14,)),
                pltpu.SemaphoreType.DMA((n,)), pltpu.SemaphoreType.DMA((n,)),
            ],
            compiler_params=pltpu.CompilerParams(
                collective_id=0, has_side_effects=True, vmem_limit_bytes=63 * 1024 * 1024),
        )(jnp.transpose(pattern, (1, 2, 3, 0)), potential.reshape(flat), charge.reshape(flat), permittivity.reshape(flat), labels.reshape(flat),
          blocks.reshape(2 * NC, A, A))
        return out.reshape(Z, X, Y), corr

    return jax.shard_map(
        per_device,
        mesh=mesh,
        in_specs=(
            P("gz", "gx", "gy"),
            P("gz", "gx", "gy"),
            P("gz", "gx", "gy"),
            P("gz", "gx", "gy"),
            P("gz", "gx", "gy", None),
            P("gz", "gx", "gy", None, None, None),
        ),
        out_specs=(P("gz", "gx", "gy"), P("gz", "gx", "gy", None)),
        check_vma=False,
    )
```

```python
import functools

import jax
import jax.numpy as jnp
from jax import lax
from jax.experimental import pallas as pl
from jax.experimental.pallas import tpu as pltpu
from jax.sharding import PartitionSpec as P

OMEGA = 0.8
CHARGE_SCALE = 40.0
COARSE_SCALE = 4.0
MESH = pl.DeviceIdType.MESH
F32 = jnp.float32
BF16 = jnp.bfloat16


def split2(value):
    high = value.astype(BF16)
    return high, (value - high.astype(F32)).astype(BF16)


def kernel(counts, Z, X, Y, A, pat_h, pot_h, chg_h, eps_h, lab_h, blk_h, swp, spread, cor,
           pat, pot, chg, eps, lab, blk, num, dia, scr, wxs, wys,
           zlo, zhi, xlo, xhi, ylo, yhi, xs_lo, xs_hi, ys,
           zlo2, zhi2, xlo2, xhi2, ylo2, yhi2, xs_lo2, xs_hi2, ys2,
           fx, zsr, zsd, weights, mine, col, choose,
           in_sem, send_sem, recv_sem, gsend, grecv):
    ids = [lax.axis_index(name) for name in ("gx", "gy", "gz")]
    CZ, CX = Z // 4, X // 4
    NC = CZ * CX
    half = Y // 2

    loads = [pltpu.make_async_copy(s, d, in_sem.at[i])
             for i, (s, d) in enumerate(((pot_h, pot), (eps_h, eps), (chg_h, chg), (lab_h, lab), (pat_h, pat), (blk_h, blk)))]
    for load in loads[:5]:
        load.start()

    def at(axis, index):
        return tuple(index if a == axis else ids[a] for a in range(3))

    def low_ok(axis):
        return ids[axis] > 0

    def high_ok(axis):
        return ids[axis] < counts[axis] - 1

    barrier = pltpu.get_barrier_semaphore()
    n = counts[0]
    for d in range(1, n):
        pl.semaphore_signal(barrier, inc=1, device_id=at(0, lax.rem(ids[0] + d, n)), device_id_type=MESH)
    expected = n - 1
    for axis in (1, 2):
        for ok, step in ((low_ok(axis), -1), (high_ok(axis), 1)):
            target = jnp.clip(ids[axis] + step, 0, counts[axis] - 1)

            @pl.when(ok)
            def _(target=target, axis=axis):
                pl.semaphore_signal(barrier, inc=1, device_id=at(axis, target), device_id_type=MESH)
            expected = expected + ok.astype(jnp.int32)

    for axis, lo_bufs, hi_bufs in ((2, (zlo, zlo2), (zhi, zhi2)), (0, (xlo, xlo2), (xhi, xhi2)), (1, (ylo, ylo2), (yhi, yhi2))):
        @pl.when(jnp.logical_not(low_ok(axis)))
        def _(bufs=lo_bufs):
            for b in bufs:
                b[...] = jnp.zeros_like(b)

        @pl.when(jnp.logical_not(high_ok(axis)))
        def _(bufs=hi_bufs):
            for b in bufs:
                b[...] = jnp.zeros_like(b)

    def up(axis, src, dst, sem):
        return (axis, True, pltpu.make_async_remote_copy(
            src_ref=src, dst_ref=dst, send_sem=send_sem.at[sem], recv_sem=recv_sem.at[sem],
            device_id=at(axis, jnp.minimum(ids[axis] + 1, counts[axis] - 1)), device_id_type=MESH))

    def down(axis, src, dst, sem):
        return (axis, False, pltpu.make_async_remote_copy(
            src_ref=src, dst_ref=dst, send_sem=send_sem.at[sem], recv_sem=recv_sem.at[sem],
            device_id=at(axis, jnp.maximum(ids[axis] - 1, 0)), device_id_type=MESH))

    def start(messages):
        for axis, upward, copy in messages:
            @pl.when(high_ok(axis) if upward else low_ok(axis))
            def _(copy=copy):
                copy.start()

    def wait_recv(messages):
        for axis, upward, copy in messages:
            @pl.when(low_ok(axis) if upward else high_ok(axis))
            def _(copy=copy):
                copy.wait_recv()

    def wait_send(messages):
        for axis, upward, copy in messages:
            @pl.when(high_ok(axis) if upward else low_ok(axis))
            def _(copy=copy):
                copy.wait_send()

    def slab(z):
        return pl.ds(pl.multiple_of(z * X, X), X)

    lane = lax.broadcasted_iota(jnp.int32, (X, 128), 1)
    pair = lane // 2
    row = lax.broadcasted_iota(jnp.int32, (X, Y), 0)
    ylane = lax.broadcasted_iota(jnp.int32, (X, Y), 1)

    def ends(value):
        return jnp.where(lane == 127, value[:, half:][:, -128:], value[:, :128])

    loads[0].wait()
    loads[1].wait()
    loads[5].start()
    def pack1(z, acc):
        acc = jnp.where(pair == z, pltpu.roll(ends(pot[slab(z), :]), 2 * z + 1, 1), acc)
        return jnp.where(pair == z + 32, pltpu.roll(ends(eps[slab(z), :]), 2 * z + 65, 1), acc)
    ys[...] = lax.fori_loop(0, Z, pack1, jnp.zeros((X, 128), F32), unroll=8)
    for z in range(Z):
        for k, field in enumerate((pot, eps)):
            xs_lo[k * Z + z:k * Z + z + 1, :] = field[z * X:z * X + 1, :]
            xs_hi[k * Z + z:k * Z + z + 1, :] = field[z * X + X - 1:z * X + X, :]
    pl.semaphore_wait(barrier, expected)
    first = pl.ds(0, X)
    last = pl.ds((Z - 1) * X, X)
    halo1 = [
        up(0, xs_hi, xlo, 0), down(0, xs_lo, xhi, 1),
        up(1, ys, ylo, 2), down(1, ys, yhi, 3),
        up(2, pot.at[last, :], zlo.at[pl.ds(0, X), :], 4), up(2, eps.at[last, :], zlo.at[pl.ds(X, X), :], 5),
        down(2, pot.at[first, :], zhi.at[pl.ds(0, X), :], 6), down(2, eps.at[first, :], zhi.at[pl.ds(X, X), :], 7),
    ]
    start(halo1)
    loads[2].wait()
    loads[3].wait()

    not_top = row < X - 1
    not_end = ylane < Y - 1

    def sweep_local(z, carry):
        fz_prev, wz_prev = carry
        v, e = pot[slab(z), :], eps[slab(z), :]
        up_z = jnp.minimum(z + 1, Z - 1)
        inside = jnp.where(z < Z - 1, 0.5, 0.0).astype(F32)
        wz = inside * (e + eps[slab(up_z), :])
        fz = wz * (v - pot[slab(up_z), :])
        wx = jnp.where(not_top, 0.5 * (e + pltpu.roll(e, X - 1, 0)), 0.0)
        fxl = wx * (v - pltpu.roll(v, X - 1, 0))
        wy = jnp.where(not_end, 0.5 * (e + pltpu.roll(e, Y - 1, 1)), 0.0)
        fyl = wy * (v - pltpu.roll(v, Y - 1, 1))
        flux = (fz - fz_prev) + (fxl - pltpu.roll(fxl, 1, 0)) + (fyl - pltpu.roll(fyl, 1, 1))
        faces = (wz + wz_prev) + (wx + pltpu.roll(wx, 1, 0)) + (wy + pltpu.roll(wy, 1, 1))
        labels = lab[slab(z), :]
        s = e * jnp.where(labels == 1, 0.05, jnp.where(labels == 2, 0.2, 0.0))
        ep, em = jnp.exp(v), jnp.exp(-v)
        wxs[slab(z), :] = wx
        wys[slab(z), :] = wy
        scr[slab(z), :] = s
        num[slab(z), :] = CHARGE_SCALE * chg[slab(z), :] - flux - s * (0.5 * (ep - em))
        dia[slab(z), :] = faces + s * (0.5 * (ep + em))
        return fz, wz
    zero = jnp.zeros((X, Y), F32)
    lax.fori_loop(0, Z, sweep_local, (zero, zero), unroll=2)

    wait_recv(halo1)
    wz_lo = 0.5 * (eps[first, :] + zlo[X:2 * X, :])
    wz_hi = 0.5 * (eps[last, :] + zhi[X:2 * X, :])
    num[first, :] = num[first, :] - wz_lo * (pot[first, :] - zlo[0:X, :])
    num[last, :] = num[last, :] - wz_hi * (pot[last, :] - zhi[0:X, :])
    dia[first, :] = dia[first, :] + wz_lo
    dia[last, :] = dia[last, :] + wz_hi
    for k, (own, halo) in enumerate(((xs_lo, xlo), (xs_hi, xhi))):
        w = 0.5 * (own[Z:2 * Z, :] + halo[Z:2 * Z, :])
        fx[2 * k * Z:(2 * k + 1) * Z, :] = w * (own[0:Z, :] - halo[0:Z, :])
        fx[(2 * k + 1) * Z:(2 * k + 2) * Z, :] = w
    even = lane % 2 == 0
    own_y = pltpu.roll(ys[...], 127, 1)
    halo_y = jnp.where(even, ylo[...], pltpu.roll(yhi[...], 126, 1))
    wy_end = 0.5 * (pltpu.roll(own_y, 64, 1) + pltpu.roll(halo_y, 64, 1))
    fy_end = wy_end * (own_y - halo_y)

    def at_ends(value):
        return jnp.concatenate([jnp.where(lane == 0, value, 0.0), jnp.where(lane == 127, value, 0.0)], axis=1)

    def sweep(zc, acc):
        total = jnp.zeros((X, Y), F32)
        for dz in range(4):
            z = zc * 4 + dz
            shift = lax.rem(128 - 2 * z, 128)
            f = at_ends(pltpu.roll(fy_end, shift, 1))
            w = at_ends(pltpu.roll(wy_end, shift, 1))
            f = f + jnp.where(row == 0, fx[pl.ds(z, 1), :], 0.0) + jnp.where(row == X - 1, fx[pl.ds(2 * Z + z, 1), :], 0.0)
            w = w + jnp.where(row == 0, fx[pl.ds(Z + z, 1), :], 0.0) + jnp.where(row == X - 1, fx[pl.ds(3 * Z + z, 1), :], 0.0)
            d = dia[slab(z), :] + w
            total = total + d
            sw = pot[slab(z), :] + OMEGA * (num[slab(z), :] - f) / d
            swp[slab(z), :] = sw
            xs_lo2[pl.ds(z, 1), :] = sw[0:1, :]
            xs_hi2[pl.ds(z, 1), :] = sw[X - 1:X, :]
            acc = jnp.where(pair == z, pltpu.roll(ends(sw), 2 * z + 1, 1), acc)
        zsd[slab(zc), :] = total
        return acc
    ys2[...] = lax.fori_loop(0, CZ, sweep, jnp.zeros((X, 128), F32))

    halo2 = [
        up(0, xs_hi2, xlo2, 8), down(0, xs_lo2, xhi2, 9),
        up(1, ys2, ylo2, 10), down(1, ys2, yhi2, 11),
        up(2, swp.at[last, :], zlo2, 12), down(2, swp.at[first, :], zhi2, 13),
    ]
    start(halo2)

    def residual_local(zc, fz_prev):
        total = jnp.zeros((X, Y), F32)
        for dz in range(4):
            z = zc * 4 + dz
            v, e = swp[slab(z), :], eps[slab(z), :]
            up_z = jnp.minimum(z + 1, Z - 1)
            inside = jnp.where(z < Z - 1, 0.5, 0.0).astype(F32)
            fz = inside * (e + eps[slab(up_z), :]) * (v - swp[slab(up_z), :])
            fxl = wxs[slab(z), :] * (v - pltpu.roll(v, X - 1, 0))
            fyl = wys[slab(z), :] * (v - pltpu.roll(v, Y - 1, 1))
            flux = (fz - fz_prev) + (fxl - pltpu.roll(fxl, 1, 0)) + (fyl - pltpu.roll(fyl, 1, 1))
            total = total + (CHARGE_SCALE * chg[slab(z), :] - flux - scr[slab(z), :] * (0.5 * (jnp.exp(v) - jnp.exp(-v))))
            fz_prev = fz
        zsr[slab(zc), :] = total
        return fz_prev
    lax.fori_loop(0, CZ, residual_local, zero)

    loads[5].wait()
    def split_blocks(zc, c):
        for xc in range(CX):
            at_block = (zc * CX + xc) * 2
            both = jnp.concatenate([blk[at_block], blk[at_block + 1]], axis=1)
            high, low = split2(both)
            here = pl.ds(pl.multiple_of(zc * A, A), A)
            weights[xc, here, 0:2 * A] = high
            weights[xc, here, 2 * A:4 * A] = low
        return c
    lax.fori_loop(0, CZ, split_blocks, 0)

    loads[4].wait()
    diagonal = lax.broadcasted_iota(jnp.int32, (CZ, CZ), 0) == lax.broadcasted_iota(jnp.int32, (CZ, CZ), 1)
    names = lax.broadcasted_iota(jnp.int32, (CZ, n * NC), 1).astype(F32)
    for k in range(2):
        for xc in range(CX):
            wanted = jnp.sum(jnp.where(diagonal, pat[xc, 0, k:k + 1, :].astype(F32), 0.0), axis=1, keepdims=True)
            at_row = (k * CX + xc) * CZ
            choose[at_row:at_row + CZ, :] = jnp.where(names == wanted, 1.0, 0.0)

    merge = jnp.where(lax.broadcasted_iota(jnp.int32, (Y, 128), 0) // 4 == lax.broadcasted_iota(jnp.int32, (Y, 128), 1) % A, 1.0, 0.0).astype(BF16)

    def coarse_rows(ref):
        groups = []
        for xc in range(CX):
            rows = []
            for zc in range(CZ):
                base = zc * X + 4 * xc
                block = ref[zc * X + (xc // 2) * 8:zc * X + (xc // 2) * 8 + 8, :]
                rows.append(jnp.sum(block[(xc % 2) * 4:(xc % 2) * 4 + 4, :], axis=0, keepdims=True))
            groups.append(jnp.concatenate(rows, axis=0))
        return groups

    def merged(groups):
        high, low = split2(jnp.concatenate(groups, axis=0))
        both = jnp.dot(jnp.concatenate([high, low], axis=0), merge, preferred_element_type=F32)
        return (both[0:NC, :] + both[NC:2 * NC, :]) * (1.0 / 64.0)

    coarse_diag = merged(coarse_rows(zsd))

    wait_recv(halo2)
    zsr[0:X, :] = zsr[0:X, :] - wz_lo * (swp[first, :] - zlo2[...])
    zsr[(CZ - 1) * X:CZ * X, :] = zsr[(CZ - 1) * X:CZ * X, :] - wz_hi * (swp[last, :] - zhi2[...])
    own_y = pltpu.roll(ys2[...], 127, 1)
    halo_y = jnp.where(even, ylo2[...], pltpu.roll(yhi2[...], 126, 1))
    f = wy_end * (own_y - halo_y)
    f = f + pltpu.roll(f, 126, 1)
    f = f + pltpu.roll(f, 124, 1)
    for zc in range(CZ):
        zsr[zc * X:(zc + 1) * X, :] = zsr[zc * X:(zc + 1) * X, :] - at_ends(pltpu.roll(f, (128 - 8 * zc) % 128, 1))
    groups = coarse_rows(zsr)
    for k, (own, halo, xc) in enumerate(((xs_lo2, xlo2, 0), (xs_hi2, xhi2, CX - 1))):
        f = fx[(2 * k + 1) * Z:(2 * k + 2) * Z, :] * (own[...] - halo[...])
        groups[xc] = groups[xc] - jnp.concatenate(
            [jnp.sum(f[4 * zc:4 * zc + 4, :], axis=0, keepdims=True) for zc in range(CZ)], axis=0)
    coarse_resid = merged(groups)
    mine[...] = coarse_resid
    my_rows = pl.ds(pl.multiple_of(ids[0] * NC, NC), NC)
    gathers = []
    for d in range(1, n):
        copy = pltpu.make_async_remote_copy(
            src_ref=mine, dst_ref=col.at[my_rows, :], send_sem=gsend.at[d - 1], recv_sem=grecv.at[d - 1],
            device_id=at(0, lax.rem(ids[0] + d, n)), device_id_type=MESH)
        copy.start()
        gathers.append(copy)
    col[my_rows, :] = coarse_resid
    for copy in gathers:
        copy.wait_recv()

    left = lax.broadcasted_iota(jnp.int32, (CZ, 128), 1) < A
    picked = jnp.dot(choose[...].astype(BF16), jnp.concatenate(split2(col[...]), axis=1), preferred_element_type=F32)
    zrow = lax.broadcasted_iota(jnp.int32, (CZ, 128), 0)
    rows = []
    for xc in range(CX):
        p0, p1 = picked[xc * CZ:(xc + 1) * CZ, :], picked[(CX + xc) * CZ:(CX + xc + 1) * CZ, :]
        high, low = [jnp.where(left, p0[:, i:i + 128], p1[:, i:i + 128]) for i in (0, 128)]
        lhs = jnp.concatenate([jnp.concatenate([high, high], axis=1),
                               jnp.concatenate([low, jnp.zeros_like(low)], axis=1)], axis=0).astype(BF16)
        prod = lax.dot_general(lhs, weights[xc], (((1,), (1,)), ((), ())), preferred_element_type=F32)
        prod = prod[0:CZ, :] + prod[CZ:2 * CZ, :]
        mine_only = jnp.zeros((CZ, 128), F32)
        for i in range(CZ // 2):
            mine_only = jnp.where(zrow // 2 == i, prod[:, i * 128:(i + 1) * 128], mine_only)
        rows.append(jnp.where(left == (zrow % 2 == 0), mine_only, pltpu.roll(mine_only, A, 1)))
    coupled = jnp.concatenate(rows, axis=0)

    correction = COARSE_SCALE * (coarse_resid + coupled) / coarse_diag
    cor[...] = correction
    high, low = split2(jnp.where(lax.broadcasted_iota(jnp.int32, (NC, 128), 1) < A, correction, 0.0))
    both = lax.dot_general(jnp.concatenate([high, low], axis=0), merge, (((1,), (1,)), ((), ())), preferred_element_type=F32)
    spread[...] = both[0:NC, :] + both[NC:2 * NC, :]
    wait_send(halo1)
    wait_send(halo2)
    for copy in gathers:
        copy.wait_send()


def finish(Z, X, Y, A, swp, spread, cor, out, corr, stage, small, sem):
    CZ, CX = Z // 4, X // 4
    for xc in range(CX):
        small[:, xc, 0, :] = cor[xc * CZ:(xc + 1) * CZ, 0:A]
    copies = [pltpu.make_async_copy(small, corr, sem.at[CZ])]
    copies[0].start()
    quarter = lax.broadcasted_iota(jnp.int32, (X, Y), 0) // 4
    for zc in range(CZ):
        add = jnp.zeros((X, Y), F32)
        for xc in range(CX):
            add = jnp.where(quarter == xc, spread[xc * CZ + zc:xc * CZ + zc + 1, :], add)
        for z in range(zc * 4, zc * 4 + 4):
            stage[z * X:(z + 1) * X, :] = swp[z * X:(z + 1) * X, :] + add
        rows = pl.ds(zc * 4 * X, 4 * X)
        copy = pltpu.make_async_copy(stage.at[rows, :], out.at[rows, :], sem.at[zc])
        copy.start()
        copies.append(copy)
    for copy in copies:
        copy.wait()


def solution(mesh):
    counts = (mesh.shape["gx"], mesh.shape["gy"], mesh.shape["gz"])

    def per_device(potential, charge, permittivity, labels, pattern, blocks):
        Z, X, Y = potential.shape
        A = blocks.shape[-1]
        CZ, CX = Z // 4, X // 4
        NC = CZ * CX
        flat = (Z * X, Y)
        whole = pltpu.VMEM(flat, F32)
        any_spec = pl.BlockSpec(memory_space=pltpu.HBM)
        vmem = pl.BlockSpec(memory_space=pltpu.VMEM)
        n = counts[0]

        def halo_scratch(k):
            return [pltpu.VMEM((k * X, Y), F32)] * 2 + [pltpu.VMEM((k * Z, Y), F32)] * 2 + [pltpu.VMEM((X, 128), F32)] * 2 + \
                [pltpu.VMEM((k * Z, Y), F32)] * 2 + [pltpu.VMEM((X, 128), F32)]

        swept, spread, cor = pl.pallas_call(
            functools.partial(kernel, counts, Z, X, Y, A),
            out_shape=(whole, pltpu.VMEM((NC, Y), F32), pltpu.VMEM((NC, 128), F32)),
            in_specs=[any_spec] * 6,
            out_specs=(vmem, vmem, vmem),
            scratch_shapes=[
                pltpu.VMEM((CX, 1, 2, CZ), jnp.int32), whole, whole, whole, pltpu.VMEM(flat, jnp.int32), pltpu.VMEM((2 * NC, A, A), F32),
                whole, whole, whole, whole, whole,
                *halo_scratch(2), *halo_scratch(1),
                pltpu.VMEM((4 * Z, Y), F32), pltpu.VMEM((CZ * X, Y), F32), pltpu.VMEM((CZ * X, Y), F32),
                pltpu.VMEM((CX, CZ * A, 4 * A), BF16), pltpu.VMEM((NC, 128), F32), pltpu.VMEM((n * NC, 128), F32),
                pltpu.VMEM((2 * NC, n * NC), F32),
                pltpu.SemaphoreType.DMA((6,)), pltpu.SemaphoreType.DMA((14,)), pltpu.SemaphoreType.DMA((14,)),
                pltpu.SemaphoreType.DMA((n,)), pltpu.SemaphoreType.DMA((n,)),
            ],
            compiler_params=pltpu.CompilerParams(
                collective_id=0, has_side_effects=True, vmem_limit_bytes=32 * 1024 * 1024),
        )(*[pltpu.with_memory_space_constraint(x, pltpu.HBM) for x in (
            jnp.transpose(pattern, (1, 2, 3, 0)), potential.reshape(flat), charge.reshape(flat), permittivity.reshape(flat),
            labels.reshape(flat), blocks.reshape(2 * NC, A, A))])
        out, corr = pl.pallas_call(
            functools.partial(finish, Z, X, Y, A),
            out_shape=(jax.ShapeDtypeStruct(flat, F32), jax.ShapeDtypeStruct((CZ, CX, 1, A), F32)),
            in_specs=[vmem] * 3,
            out_specs=(any_spec, any_spec),
            scratch_shapes=[whole, pltpu.VMEM((CZ, CX, 1, A), F32), pltpu.SemaphoreType.DMA((CZ + 1,))],
            compiler_params=pltpu.CompilerParams(vmem_limit_bytes=32 * 1024 * 1024),
        )(swept, spread, cor)
        return out.reshape(Z, X, Y), corr

    return jax.shard_map(
        per_device,
        mesh=mesh,
        in_specs=(
            P("gz", "gx", "gy"),
            P("gz", "gx", "gy"),
            P("gz", "gx", "gy"),
            P("gz", "gx", "gy"),
            P("gz", "gx", "gy", None),
            P("gz", "gx", "gy", None, None, None),
        ),
        out_specs=(P("gz", "gx", "gy"), P("gz", "gx", "gy", None)),
        check_vma=False,
    )
```

```python
import functools

import jax
import jax.numpy as jnp
from jax import lax
from jax.experimental import pallas as pl
from jax.experimental.pallas import tpu as pltpu
from jax.sharding import PartitionSpec as P

OMEGA = 0.8
CHARGE_SCALE = 40.0
COARSE_SCALE = 4.0
MESH = pl.DeviceIdType.MESH
F32 = jnp.float32
BF16 = jnp.bfloat16


def split2(value):
    high = value.astype(BF16)
    return high, (value - high.astype(F32)).astype(BF16)


def kernel(counts, Z, X, Y, A, pat_h, pot_h, chg_h, eps_h, lab_h, blk_h, swp, spread, cor,
           pat, pot, chg, eps, lab, blk, num, dia, scr, wxs, wys,
           zlo, zhi, xlo, xhi, ylo, yhi, xs_lo, xs_hi, ys,
           xs_lo2, xs_hi2, fx, zsr, zsd, weights, mine, zsend_lo, zsend_hi, ysend, col, parts, zin_lo, zin_hi, yin_lo, yin_hi, choose,
           in_sem, send_sem, recv_sem, gsend, grecv):
    ids = [lax.axis_index(name) for name in ("gx", "gy", "gz")]
    CZ, CX = Z // 4, X // 4
    NC = CZ * CX
    half = Y // 2

    loads = [pltpu.make_async_copy(s, d, in_sem.at[i])
             for i, (s, d) in enumerate(((pot_h, pot), (eps_h, eps), (chg_h, chg), (lab_h, lab), (pat_h, pat), (blk_h, blk)))]
    for load in loads[:5]:
        load.start()

    def at(axis, index):
        return tuple(index if a == axis else ids[a] for a in range(3))

    def low_ok(axis):
        return ids[axis] > 0

    def high_ok(axis):
        return ids[axis] < counts[axis] - 1

    barrier = pltpu.get_barrier_semaphore()
    n = counts[0]

    def peer(d, axis=0, step=0):
        target = list(ids)
        if axis:
            target[axis] = jnp.clip(ids[axis] + step, 0, counts[axis] - 1)
        target[0] = lax.rem(ids[0] + d, n)
        return tuple(target)

    for d in range(1, n):
        pl.semaphore_signal(barrier, inc=1, device_id=peer(d), device_id_type=MESH)
    expected = n - 1
    for axis in (1, 2):
        for ok, step in ((low_ok(axis), -1), (high_ok(axis), 1)):
            @pl.when(ok)
            def _(axis=axis, step=step):
                for d in range(n):
                    pl.semaphore_signal(barrier, inc=1, device_id=peer(d, axis, step), device_id_type=MESH)
            expected = expected + n * ok.astype(jnp.int32)

    for axis, lo_bufs, hi_bufs in ((2, (zlo, zin_lo), (zhi, zin_hi)), (0, (xlo,), (xhi,)), (1, (ylo, yin_lo), (yhi, yin_hi))):
        @pl.when(jnp.logical_not(low_ok(axis)))
        def _(bufs=lo_bufs):
            for b in bufs:
                b[...] = jnp.zeros_like(b)

        @pl.when(jnp.logical_not(high_ok(axis)))
        def _(bufs=hi_bufs):
            for b in bufs:
                b[...] = jnp.zeros_like(b)

    def up(axis, src, dst, sem):
        return (axis, True, pltpu.make_async_remote_copy(
            src_ref=src, dst_ref=dst, send_sem=send_sem.at[sem], recv_sem=recv_sem.at[sem],
            device_id=at(axis, jnp.minimum(ids[axis] + 1, counts[axis] - 1)), device_id_type=MESH))

    def down(axis, src, dst, sem):
        return (axis, False, pltpu.make_async_remote_copy(
            src_ref=src, dst_ref=dst, send_sem=send_sem.at[sem], recv_sem=recv_sem.at[sem],
            device_id=at(axis, jnp.maximum(ids[axis] - 1, 0)), device_id_type=MESH))

    def start(messages):
        for axis, upward, copy in messages:
            @pl.when(high_ok(axis) if upward else low_ok(axis))
            def _(copy=copy):
                copy.start()

    def wait_recv(messages):
        for axis, upward, copy in messages:
            @pl.when(low_ok(axis) if upward else high_ok(axis))
            def _(copy=copy):
                copy.wait_recv()

    def wait_send(messages):
        for axis, upward, copy in messages:
            @pl.when(high_ok(axis) if upward else low_ok(axis))
            def _(copy=copy):
                copy.wait_send()

    def slab(z):
        return pl.ds(pl.multiple_of(z * X, X), X)

    lane = lax.broadcasted_iota(jnp.int32, (X, 128), 1)
    pair = lane // 2
    row = lax.broadcasted_iota(jnp.int32, (X, Y), 0)
    ylane = lax.broadcasted_iota(jnp.int32, (X, Y), 1)

    def ends(value):
        return jnp.where(lane == 127, value[:, half:][:, -128:], value[:, :128])

    loads[0].wait()
    loads[1].wait()
    loads[5].start()
    for z in range(Z):
        for k, field in enumerate((pot, eps)):
            xs_lo[k * Z + z:k * Z + z + 1, :] = field[z * X:z * X + 1, :]
            xs_hi[k * Z + z:k * Z + z + 1, :] = field[z * X + X - 1:z * X + X, :]
    pl.semaphore_wait(barrier, expected)
    first = pl.ds(0, X)
    last = pl.ds((Z - 1) * X, X)
    halo1 = [
        up(0, xs_hi, xlo, 0), down(0, xs_lo, xhi, 1),
        up(2, pot.at[last, :], zlo.at[pl.ds(0, X), :], 4), up(2, eps.at[last, :], zlo.at[pl.ds(X, X), :], 5),
        down(2, pot.at[first, :], zhi.at[pl.ds(0, X), :], 6), down(2, eps.at[first, :], zhi.at[pl.ds(X, X), :], 7),
        up(1, ys, ylo, 2), down(1, ys, yhi, 3),
    ]
    start(halo1[:6])
    def pack1(z, acc):
        acc = jnp.where(pair == z, pltpu.roll(ends(pot[slab(z), :]), 2 * z + 1, 1), acc)
        return jnp.where(pair == z + 32, pltpu.roll(ends(eps[slab(z), :]), 2 * z + 65, 1), acc)
    ys[...] = lax.fori_loop(0, Z, pack1, jnp.zeros((X, 128), F32), unroll=8)
    start(halo1[6:])
    loads[2].wait()
    loads[3].wait()

    not_top = row < X - 1
    not_end = ylane < Y - 1

    def sweep_local(z, carry):
        fz_prev, wz_prev = carry
        v, e = pot[slab(z), :], eps[slab(z), :]
        up_z = jnp.minimum(z + 1, Z - 1)
        inside = jnp.where(z < Z - 1, 0.5, 0.0).astype(F32)
        wz = inside * (e + eps[slab(up_z), :])
        fz = wz * (v - pot[slab(up_z), :])
        wx = jnp.where(not_top, 0.5 * (e + pltpu.roll(e, X - 1, 0)), 0.0)
        fxl = wx * (v - pltpu.roll(v, X - 1, 0))
        wy = jnp.where(not_end, 0.5 * (e + pltpu.roll(e, Y - 1, 1)), 0.0)
        fyl = wy * (v - pltpu.roll(v, Y - 1, 1))
        flux = (fz - fz_prev) + (fxl - pltpu.roll(fxl, 1, 0)) + (fyl - pltpu.roll(fyl, 1, 1))
        faces = (wz + wz_prev) + (wx + pltpu.roll(wx, 1, 0)) + (wy + pltpu.roll(wy, 1, 1))
        labels = lab[slab(z), :]
        s = e * jnp.where(labels == 1, 0.05, jnp.where(labels == 2, 0.2, 0.0))
        ep, em = jnp.exp(v), jnp.exp(-v)
        wxs[slab(z), :] = wx
        wys[slab(z), :] = wy
        scr[slab(z), :] = s
        num[slab(z), :] = CHARGE_SCALE * chg[slab(z), :] - flux - s * (0.5 * (ep - em))
        dia[slab(z), :] = faces + s * (0.5 * (ep + em))
        return fz, wz
    zero = jnp.zeros((X, Y), F32)
    lax.fori_loop(0, Z, sweep_local, (zero, zero), unroll=4)

    wait_recv(halo1)
    wz_lo = 0.5 * (eps[first, :] + zlo[X:2 * X, :])
    wz_hi = 0.5 * (eps[last, :] + zhi[X:2 * X, :])
    num[first, :] = num[first, :] - wz_lo * (pot[first, :] - zlo[0:X, :])
    num[last, :] = num[last, :] - wz_hi * (pot[last, :] - zhi[0:X, :])
    dia[first, :] = dia[first, :] + wz_lo
    dia[last, :] = dia[last, :] + wz_hi
    for k, (own, halo) in enumerate(((xs_lo, xlo), (xs_hi, xhi))):
        w = 0.5 * (own[Z:2 * Z, :] + halo[Z:2 * Z, :])
        fx[2 * k * Z:(2 * k + 1) * Z, :] = w * (own[0:Z, :] - halo[0:Z, :])
        fx[(2 * k + 1) * Z:(2 * k + 2) * Z, :] = w
    even = lane % 2 == 0
    own_y = pltpu.roll(ys[...], 127, 1)
    halo_y = jnp.where(even, ylo[...], pltpu.roll(yhi[...], 126, 1))
    wy_end = 0.5 * (pltpu.roll(own_y, 64, 1) + pltpu.roll(halo_y, 64, 1))
    fy_end = wy_end * (own_y - halo_y)

    def at_ends(value):
        return jnp.concatenate([jnp.where(lane == 0, value, 0.0), jnp.where(lane == 127, value, 0.0)], axis=1)

    row8 = lax.broadcasted_iota(jnp.int32, (X // 2, Y), 0)

    def at_rows(low, high):
        return jnp.concatenate([jnp.where(row8 == 0, low, 0.0), jnp.where(row8 == X // 2 - 1, high, 0.0)], axis=0)

    def sweep(zc, acc):
        total = jnp.zeros((X, Y), F32)
        for dz in range(4):
            z = zc * 4 + dz
            shift = lax.rem(128 - 2 * z, 128)
            f = at_ends(pltpu.roll(fy_end, shift, 1))
            w = at_ends(pltpu.roll(wy_end, shift, 1))
            f = f + at_rows(fx[pl.ds(z, 1), :], fx[pl.ds(2 * Z + z, 1), :])
            w = w + at_rows(fx[pl.ds(Z + z, 1), :], fx[pl.ds(3 * Z + z, 1), :])
            d = dia[slab(z), :] + w
            total = total + d
            sw = pot[slab(z), :] + OMEGA * (num[slab(z), :] - f) / d
            swp[slab(z), :] = sw
            xs_lo2[pl.ds(z, 1), :] = sw[0:1, :]
            xs_hi2[pl.ds(z, 1), :] = sw[X - 1:X, :]
            acc = jnp.where(pair == z, pltpu.roll(ends(sw), 2 * z + 1, 1), acc)
        zsd[slab(zc), :] = total
        return acc
    ys2 = lax.fori_loop(0, CZ, sweep, jnp.zeros((X, 128), F32), unroll=4)

    def residual_local(zc, fz_prev):
        total = jnp.zeros((X, Y), F32)
        for dz in range(4):
            z = zc * 4 + dz
            v, e = swp[slab(z), :], eps[slab(z), :]
            up_z = jnp.minimum(z + 1, Z - 1)
            inside = jnp.where(z < Z - 1, 0.5, 0.0).astype(F32)
            fz = inside * (e + eps[slab(up_z), :]) * (v - swp[slab(up_z), :])
            fxl = wxs[slab(z), :] * (v - pltpu.roll(v, X - 1, 0))
            fyl = wys[slab(z), :] * (v - pltpu.roll(v, Y - 1, 1))
            flux = (fz - fz_prev) + (fxl - pltpu.roll(fxl, 1, 0)) + (fyl - pltpu.roll(fyl, 1, 1))
            total = total + (CHARGE_SCALE * chg[slab(z), :] - flux - scr[slab(z), :] * (0.5 * (jnp.exp(v) - jnp.exp(-v))))
            fz_prev = fz
        zsr[slab(zc), :] = total
        return fz_prev
    lax.fori_loop(0, CZ, residual_local, zero, unroll=2)

    merge = jnp.where(lax.broadcasted_iota(jnp.int32, (Y, 128), 0) // 4 == lax.broadcasted_iota(jnp.int32, (Y, 128), 1) % A, 1.0, 0.0).astype(BF16)

    def coarse_rows(ref):
        groups = []
        for xc in range(CX):
            rows = []
            for zc in range(CZ):
                base = zc * X + 4 * xc
                block = ref[zc * X + (xc // 2) * 8:zc * X + (xc // 2) * 8 + 8, :]
                rows.append(jnp.sum(block[(xc % 2) * 4:(xc % 2) * 4 + 4, :], axis=0, keepdims=True))
            groups.append(jnp.concatenate(rows, axis=0))
        return groups

    def merged(groups):
        high, low = split2(jnp.concatenate(groups, axis=0))
        both = jnp.dot(jnp.concatenate([high, low], axis=0), merge, preferred_element_type=F32)
        return (both[0:high.shape[0], :] + both[high.shape[0]:, :]) * (1.0 / 64.0)

    z_lo, z_hi = wz_lo * swp[first, :], wz_hi * swp[last, :]
    zsr[0:X, :] = zsr[0:X, :] - z_lo
    zsr[(CZ - 1) * X:CZ * X, :] = zsr[(CZ - 1) * X:CZ * X, :] - z_hi
    f = wy_end * pltpu.roll(ys2, 127, 1)
    f = f + pltpu.roll(f, 126, 1)
    f = f + pltpu.roll(f, 124, 1)
    for zc in range(CZ):
        zsr[zc * X:(zc + 1) * X, :] = zsr[zc * X:(zc + 1) * X, :] - at_ends(pltpu.roll(f, (128 - 8 * zc) % 128, 1))
    groups = coarse_rows(zsr)

    def sum_rows(value):
        return jnp.concatenate([jnp.sum(value[i:i + 4, :], axis=0, keepdims=True) for i in range(0, value.shape[0], 4)], axis=0)

    x_lo, x_hi = sum_rows(fx[Z:2 * Z, :] * xs_lo2[...]), sum_rows(fx[3 * Z:4 * Z, :] * xs_hi2[...])
    groups[0] = groups[0] - x_lo
    groups[-1] = groups[-1] - x_hi
    z_sums = jnp.concatenate([sum_rows(z_lo), sum_rows(z_hi)], axis=0)
    both = merged(groups + [x_lo, x_hi, z_sums, jnp.zeros_like(z_sums)])
    ROWS = NC + 2 * CZ
    mine[...] = both[0:ROWS, :]
    zsend_lo[0:CX, :] = both[ROWS:ROWS + CX, :]
    zsend_hi[0:CX, :] = both[ROWS + CX:ROWS + 2 * CX, :]
    ysend[0:CX, :] = sum_rows(f) * (1.0 / 64.0)
    for ref in (zsend_lo, zsend_hi, ysend):
        ref[CX:8, :] = jnp.zeros((8 - CX, 128), F32)

    def to_peer(src, dst, lane_of_sem, d, axis, step):
        return pltpu.make_async_remote_copy(
            src_ref=src, dst_ref=dst, send_sem=gsend.at[lane_of_sem * n + d], recv_sem=grecv.at[lane_of_sem * n + d],
            device_id=peer(d, axis, step), device_id_type=MESH)

    at_mine = pl.ds(pl.multiple_of(ids[0] * ROWS, 16), ROWS)
    at_eight = pl.ds(pl.multiple_of(ids[0] * 8, 8), 8)
    shares = []
    for kind, (axis, step, src, dst) in enumerate(((1, 1, ysend, yin_lo), (1, -1, ysend, yin_hi), (2, 1, zsend_hi, zin_lo), (2, -1, zsend_lo, zin_hi))):
        shares.append((axis, step == 1, [to_peer(src, dst.at[at_eight, :], kind + 1, d, axis, step) for d in range(n)]))
    gathers = [to_peer(mine, parts.at[at_mine, :], 0, d, 0, 0) for d in range(1, n)]
    for copy in gathers:
        copy.start()
    for axis, upward, copies in shares:
        @pl.when(high_ok(axis) if upward else low_ok(axis))
        def _(copies=copies):
            for copy in copies:
                copy.start()
    parts[at_mine, :] = both[0:ROWS, :]

    loads[5].wait()
    def split_blocks(zc, c):
        for xc in range(CX):
            at_block = (zc * CX + xc) * 2
            both = jnp.concatenate([blk[at_block], blk[at_block + 1]], axis=1)
            high, low = split2(both)
            here = pl.ds(pl.multiple_of(zc * A, A), A)
            weights[xc, here, 0:2 * A] = high
            weights[xc, here, 2 * A:4 * A] = low
        return c
    lax.fori_loop(0, CZ, split_blocks, 0)

    loads[4].wait()
    diagonal = lax.broadcasted_iota(jnp.int32, (CZ, CZ), 0) == lax.broadcasted_iota(jnp.int32, (CZ, CZ), 1)
    names = lax.broadcasted_iota(jnp.int32, (CZ, n * NC), 1).astype(F32)
    for k in range(2):
        for xc in range(CX):
            wanted = jnp.sum(jnp.where(diagonal, pat[xc, 0, k:k + 1, :].astype(F32), 0.0), axis=1, keepdims=True)
            at_row = (k * CX + xc) * CZ
            choose[at_row:at_row + CZ, :] = jnp.where(names == wanted, 1.0, 0.0)

    coarse_diag = merged(coarse_rows(zsd))

    for copy in gathers:
        copy.wait_recv()
    for axis, upward, copies in shares:
        @pl.when(low_ok(axis) if upward else high_ok(axis))
        def _(copies=copies):
            for copy in copies:
                copy.wait_recv()
    sub8 = lax.broadcasted_iota(jnp.int32, (CZ, 128), 0)
    lane8 = lax.broadcasted_iota(jnp.int32, (CZ, 128), 1)
    low_lane, high_lane = lane8 == 8 * sub8, lane8 == (8 * sub8 + 127) % 128
    first_cell, last_cell = lane8 % A == 0, lane8 % A == A - 1
    for g in range(n):
        for xc in range(CX):
            b = parts[g * ROWS + xc * CZ:g * ROWS + (xc + 1) * CZ, :]
            if xc == 0 and g > 0:
                b = b + parts[(g - 1) * ROWS + NC + CZ:g * ROWS, :]
            if xc == CX - 1 and g < n - 1:
                b = b + parts[(g + 1) * ROWS + NC:(g + 1) * ROWS + NC + CZ, :]
            here = slice(g * 8 + xc, g * 8 + xc + 1)
            b = b + jnp.where(sub8 == 0, zin_lo[here, :], 0.0) + jnp.where(sub8 == CZ - 1, zin_hi[here, :], 0.0)
            from_low = jnp.sum(jnp.where(high_lane, yin_lo[here, :], 0.0), axis=1, keepdims=True)
            from_high = jnp.sum(jnp.where(low_lane, yin_hi[here, :], 0.0), axis=1, keepdims=True)
            b = b + jnp.where(first_cell, from_low, 0.0) + jnp.where(last_cell, from_high, 0.0)
            col[g * NC + xc * CZ:g * NC + (xc + 1) * CZ, :] = b
    coarse_resid = col[pl.ds(pl.multiple_of(ids[0] * NC, NC), NC), :]

    left = lax.broadcasted_iota(jnp.int32, (CZ, 128), 1) < A
    picked = jnp.dot(choose[...].astype(BF16), jnp.concatenate(split2(col[...]), axis=1), preferred_element_type=F32)
    zrow = lax.broadcasted_iota(jnp.int32, (CZ, 128), 0)
    rows = []
    for xc in range(CX):
        p0, p1 = picked[xc * CZ:(xc + 1) * CZ, :], picked[(CX + xc) * CZ:(CX + xc + 1) * CZ, :]
        high, low = [jnp.where(left, p0[:, i:i + 128], p1[:, i:i + 128]) for i in (0, 128)]
        lhs = jnp.concatenate([jnp.concatenate([high, high], axis=1),
                               jnp.concatenate([low, jnp.zeros_like(low)], axis=1)], axis=0).astype(BF16)
        prod = lax.dot_general(lhs, weights[xc], (((1,), (1,)), ((), ())), preferred_element_type=F32)
        prod = prod[0:CZ, :] + prod[CZ:2 * CZ, :]
        mine_only = jnp.zeros((CZ, 128), F32)
        for i in range(CZ // 2):
            mine_only = jnp.where(zrow // 2 == i, prod[:, i * 128:(i + 1) * 128], mine_only)
        rows.append(jnp.where(left == (zrow % 2 == 0), mine_only, pltpu.roll(mine_only, A, 1)))
    coupled = jnp.concatenate(rows, axis=0)

    correction = COARSE_SCALE * (coarse_resid + coupled) / coarse_diag
    cor[...] = correction
    high, low = split2(jnp.where(lax.broadcasted_iota(jnp.int32, (NC, 128), 1) < A, correction, 0.0))
    both = lax.dot_general(jnp.concatenate([high, low], axis=0), merge, (((1,), (1,)), ((), ())), preferred_element_type=F32)
    spread[...] = both[0:NC, :] + both[NC:2 * NC, :]
    wait_send(halo1)
    for copy in gathers:
        copy.wait_send()
    for axis, upward, copies in shares:
        @pl.when(high_ok(axis) if upward else low_ok(axis))
        def _(copies=copies):
            for copy in copies:
                copy.wait_send()


def finish(Z, X, Y, A, swp, spread, cor, out, corr, stage, small, sem):
    CZ, CX = Z // 4, X // 4
    for xc in range(CX):
        small[:, xc, 0, :] = cor[xc * CZ:(xc + 1) * CZ, 0:A]
    copies = [pltpu.make_async_copy(small, corr, sem.at[CZ])]
    copies[0].start()
    quarter = lax.broadcasted_iota(jnp.int32, (X, Y), 0) // 4
    for zc in range(CZ):
        add = jnp.zeros((X, Y), F32)
        for xc in range(CX):
            add = jnp.where(quarter == xc, spread[xc * CZ + zc:xc * CZ + zc + 1, :], add)
        for z in range(zc * 4, zc * 4 + 4):
            stage[z * X:(z + 1) * X, :] = swp[z * X:(z + 1) * X, :] + add
        rows = pl.ds(zc * 4 * X, 4 * X)
        copy = pltpu.make_async_copy(stage.at[rows, :], out.at[rows, :], sem.at[zc])
        copy.start()
        copies.append(copy)
    for copy in copies:
        copy.wait()


def solution(mesh):
    counts = (mesh.shape["gx"], mesh.shape["gy"], mesh.shape["gz"])

    def per_device(potential, charge, permittivity, labels, pattern, blocks):
        Z, X, Y = potential.shape
        A = blocks.shape[-1]
        CZ, CX = Z // 4, X // 4
        NC = CZ * CX
        flat = (Z * X, Y)
        whole = pltpu.VMEM(flat, F32)
        any_spec = pl.BlockSpec(memory_space=pltpu.HBM)
        vmem = pl.BlockSpec(memory_space=pltpu.VMEM)
        n = counts[0]

        swept, spread, cor = pl.pallas_call(
            functools.partial(kernel, counts, Z, X, Y, A),
            out_shape=(whole, pltpu.VMEM((NC, Y), F32), pltpu.VMEM((NC, 128), F32)),
            in_specs=[any_spec] * 6,
            out_specs=(vmem, vmem, vmem),
            scratch_shapes=[
                pltpu.VMEM((CX, 1, 2, CZ), jnp.int32), whole, whole, whole, pltpu.VMEM(flat, jnp.int32), pltpu.VMEM((2 * NC, A, A), F32),
                whole, whole, whole, whole, whole,
                *[pltpu.VMEM((2 * X, Y), F32)] * 2, *[pltpu.VMEM((2 * Z, Y), F32)] * 2, *[pltpu.VMEM((X, 128), F32)] * 2,
                *[pltpu.VMEM((2 * Z, Y), F32)] * 2, pltpu.VMEM((X, 128), F32),
                *[pltpu.VMEM((Z, Y), F32)] * 2,
                pltpu.VMEM((4 * Z, Y), F32), pltpu.VMEM((CZ * X, Y), F32), pltpu.VMEM((CZ * X, Y), F32),
                pltpu.VMEM((CX, CZ * A, 4 * A), BF16), pltpu.VMEM((NC + 2 * CZ, 128), F32), *[pltpu.VMEM((8, 128), F32)] * 3,
                pltpu.VMEM((n * NC, 128), F32), pltpu.VMEM((n * (NC + 2 * CZ), 128), F32), *[pltpu.VMEM((n * 8, 128), F32)] * 4,
                pltpu.VMEM((2 * NC, n * NC), F32),
                pltpu.SemaphoreType.DMA((6,)), pltpu.SemaphoreType.DMA((8,)), pltpu.SemaphoreType.DMA((8,)),
                pltpu.SemaphoreType.DMA((5 * n,)), pltpu.SemaphoreType.DMA((5 * n,)),
            ],
            compiler_params=pltpu.CompilerParams(
                collective_id=0, has_side_effects=True, vmem_limit_bytes=32 * 1024 * 1024),
        )(*[pltpu.with_memory_space_constraint(x, pltpu.HBM) for x in (
            jnp.transpose(pattern, (1, 2, 3, 0)), potential.reshape(flat), charge.reshape(flat), permittivity.reshape(flat),
            labels.reshape(flat), blocks.reshape(2 * NC, A, A))])
        out, corr = pl.pallas_call(
            functools.partial(finish, Z, X, Y, A),
            out_shape=(jax.ShapeDtypeStruct(flat, F32), jax.ShapeDtypeStruct((CZ, CX, 1, A), F32)),
            in_specs=[vmem] * 3,
            out_specs=(any_spec, any_spec),
            scratch_shapes=[whole, pltpu.VMEM((CZ, CX, 1, A), F32), pltpu.SemaphoreType.DMA((CZ + 1,))],
            compiler_params=pltpu.CompilerParams(vmem_limit_bytes=32 * 1024 * 1024),
        )(swept, spread, cor)
        return out.reshape(Z, X, Y), corr

    return jax.shard_map(
        per_device,
        mesh=mesh,
        in_specs=(
            P("gz", "gx", "gy"),
            P("gz", "gx", "gy"),
            P("gz", "gx", "gy"),
            P("gz", "gx", "gy"),
            P("gz", "gx", "gy", None),
            P("gz", "gx", "gy", None, None, None),
        ),
        out_specs=(P("gz", "gx", "gy"), P("gz", "gx", "gy", None)),
        check_vma=False,
    )
```

```python
import functools

import jax
import jax.numpy as jnp
from jax import lax
from jax.experimental import pallas as pl
from jax.experimental.pallas import tpu as pltpu
from jax.sharding import PartitionSpec as P

OMEGA = 0.8
CHARGE_SCALE = 40.0
COARSE_SCALE = 4.0
MESH = pl.DeviceIdType.MESH
F32 = jnp.float32
BF16 = jnp.bfloat16


def split2(value):
    high = value.astype(BF16)
    return high, (value - high.astype(F32)).astype(BF16)


def kernel(counts, Z, X, Y, A, pat_h, pot_h, chg_h, eps_h, lab_h, blk_h, swp, spread, cor,
           pat, pot, chg, eps, lab, blk, num, dia, scr, wxs, wys,
           zlo, zhi, xlo, xhi, ylo, yhi, xs_lo, xs_hi, ys,
           xs_lo2, xs_hi2, fx, zsr, zsd, weights, mine, zsend_lo, zsend_hi, ysend, col, parts, zin_lo, zin_hi, yin_lo, yin_hi, choose,
           in_sem, send_sem, recv_sem, gsend, grecv):
    ids = [lax.axis_index(name) for name in ("gx", "gy", "gz")]
    CZ, CX = Z // 4, X // 4
    NC = CZ * CX
    half = Y // 2

    loads = [pltpu.make_async_copy(s, d, in_sem.at[i])
             for i, (s, d) in enumerate(((pot_h, pot), (eps_h, eps), (chg_h, chg), (lab_h, lab), (pat_h, pat), (blk_h, blk)))]
    for load in loads[:5]:
        load.start()

    def at(axis, index):
        return tuple(index if a == axis else ids[a] for a in range(3))

    def low_ok(axis):
        return ids[axis] > 0

    def high_ok(axis):
        return ids[axis] < counts[axis] - 1

    barrier = pltpu.get_barrier_semaphore()
    n = counts[0]

    def peer(d, axis=0, step=0):
        target = list(ids)
        if axis:
            target[axis] = jnp.clip(ids[axis] + step, 0, counts[axis] - 1)
        target[0] = lax.rem(ids[0] + d, n)
        return tuple(target)

    for d in range(1, n):
        pl.semaphore_signal(barrier, inc=1, device_id=peer(d), device_id_type=MESH)
    expected = n - 1
    for axis in (1, 2):
        for ok, step in ((low_ok(axis), -1), (high_ok(axis), 1)):
            @pl.when(ok)
            def _(axis=axis, step=step):
                pl.semaphore_signal(barrier, inc=1, device_id=peer(0, axis, step), device_id_type=MESH)
            expected = expected + ok.astype(jnp.int32)

    for axis, lo_bufs, hi_bufs in ((2, (zlo, zin_lo), (zhi, zin_hi)), (0, (xlo,), (xhi,)), (1, (ylo, yin_lo), (yhi, yin_hi))):
        @pl.when(jnp.logical_not(low_ok(axis)))
        def _(bufs=lo_bufs):
            for b in bufs:
                b[...] = jnp.zeros_like(b)

        @pl.when(jnp.logical_not(high_ok(axis)))
        def _(bufs=hi_bufs):
            for b in bufs:
                b[...] = jnp.zeros_like(b)

    def up(axis, src, dst, sem):
        return (axis, True, pltpu.make_async_remote_copy(
            src_ref=src, dst_ref=dst, send_sem=send_sem.at[sem], recv_sem=recv_sem.at[sem],
            device_id=at(axis, jnp.minimum(ids[axis] + 1, counts[axis] - 1)), device_id_type=MESH))

    def down(axis, src, dst, sem):
        return (axis, False, pltpu.make_async_remote_copy(
            src_ref=src, dst_ref=dst, send_sem=send_sem.at[sem], recv_sem=recv_sem.at[sem],
            device_id=at(axis, jnp.maximum(ids[axis] - 1, 0)), device_id_type=MESH))

    def start(messages):
        for axis, upward, copy in messages:
            @pl.when(high_ok(axis) if upward else low_ok(axis))
            def _(copy=copy):
                copy.start()

    def wait_recv(messages):
        for axis, upward, copy in messages:
            @pl.when(low_ok(axis) if upward else high_ok(axis))
            def _(copy=copy):
                copy.wait_recv()

    def wait_send(messages):
        for axis, upward, copy in messages:
            @pl.when(high_ok(axis) if upward else low_ok(axis))
            def _(copy=copy):
                copy.wait_send()

    def slab(z):
        return pl.ds(pl.multiple_of(z * X, X), X)

    lane = lax.broadcasted_iota(jnp.int32, (X, 128), 1)
    pair = lane // 2
    row = lax.broadcasted_iota(jnp.int32, (X, Y), 0)
    ylane = lax.broadcasted_iota(jnp.int32, (X, Y), 1)

    def ends(value):
        return jnp.where(lane == 127, value[:, half:][:, -128:], value[:, :128])

    loads[0].wait()
    loads[1].wait()
    loads[5].start()
    for z in range(Z):
        for k, field in enumerate((pot, eps)):
            xs_lo[k * Z + z:k * Z + z + 1, :] = field[z * X:z * X + 1, :]
            xs_hi[k * Z + z:k * Z + z + 1, :] = field[z * X + X - 1:z * X + X, :]
    pl.semaphore_wait(barrier, expected)
    first = pl.ds(0, X)
    last = pl.ds((Z - 1) * X, X)
    halo1 = [
        up(0, xs_hi, xlo, 0), down(0, xs_lo, xhi, 1),
        up(2, pot.at[last, :], zlo.at[pl.ds(0, X), :], 4), up(2, eps.at[last, :], zlo.at[pl.ds(X, X), :], 5),
        down(2, pot.at[first, :], zhi.at[pl.ds(0, X), :], 6), down(2, eps.at[first, :], zhi.at[pl.ds(X, X), :], 7),
        up(1, ys, ylo, 2), down(1, ys, yhi, 3),
    ]
    start(halo1[:6])
    def pack1(z, acc):
        acc = jnp.where(pair == z, pltpu.roll(ends(pot[slab(z), :]), 2 * z + 1, 1), acc)
        return jnp.where(pair == z + 32, pltpu.roll(ends(eps[slab(z), :]), 2 * z + 65, 1), acc)
    ys[...] = lax.fori_loop(0, Z, pack1, jnp.zeros((X, 128), F32), unroll=8)
    start(halo1[6:])
    loads[2].wait()
    loads[3].wait()

    not_top = row < X - 1
    not_end = ylane < Y - 1

    def sweep_local(z, carry):
        fz_prev, wz_prev = carry
        v, e = pot[slab(z), :], eps[slab(z), :]
        up_z = jnp.minimum(z + 1, Z - 1)
        inside = jnp.where(z < Z - 1, 0.5, 0.0).astype(F32)
        wz = inside * (e + eps[slab(up_z), :])
        fz = wz * (v - pot[slab(up_z), :])
        wx = jnp.where(not_top, 0.5 * (e + pltpu.roll(e, X - 1, 0)), 0.0)
        fxl = wx * (v - pltpu.roll(v, X - 1, 0))
        wy = jnp.where(not_end, 0.5 * (e + pltpu.roll(e, Y - 1, 1)), 0.0)
        fyl = wy * (v - pltpu.roll(v, Y - 1, 1))
        flux = (fz - fz_prev) + (fxl - pltpu.roll(fxl, 1, 0)) + (fyl - pltpu.roll(fyl, 1, 1))
        faces = (wz + wz_prev) + (wx + pltpu.roll(wx, 1, 0)) + (wy + pltpu.roll(wy, 1, 1))
        labels = lab[slab(z), :]
        s = e * jnp.where(labels == 1, 0.05, jnp.where(labels == 2, 0.2, 0.0))
        ep, em = jnp.exp(v), jnp.exp(-v)
        wxs[slab(z), :] = wx
        wys[slab(z), :] = wy
        scr[slab(z), :] = s
        num[slab(z), :] = CHARGE_SCALE * chg[slab(z), :] - flux - s * (0.5 * (ep - em))
        dia[slab(z), :] = faces + s * (0.5 * (ep + em))
        return fz, wz
    zero = jnp.zeros((X, Y), F32)
    lax.fori_loop(0, Z, sweep_local, (zero, zero), unroll=4)

    loads[5].wait()
    def split_blocks(zc, c):
        for xc in range(CX):
            at_block = (zc * CX + xc) * 2
            both = jnp.concatenate([blk[at_block], blk[at_block + 1]], axis=1)
            high, low = split2(both)
            here = pl.ds(pl.multiple_of(zc * A, A), A)
            weights[xc, here, 0:2 * A] = high
            weights[xc, here, 2 * A:4 * A] = low
        return c
    lax.fori_loop(0, CZ, split_blocks, 0)

    loads[4].wait()
    diagonal = lax.broadcasted_iota(jnp.int32, (CZ, CZ), 0) == lax.broadcasted_iota(jnp.int32, (CZ, CZ), 1)
    names = lax.broadcasted_iota(jnp.int32, (CZ, n * NC), 1).astype(F32)
    for k in range(2):
        for xc in range(CX):
            wanted = jnp.sum(jnp.where(diagonal, pat[xc, 0, k:k + 1, :].astype(F32), 0.0), axis=1, keepdims=True)
            at_row = (k * CX + xc) * CZ
            choose[at_row:at_row + CZ, :] = jnp.where(names == wanted, 1.0, 0.0)

    wait_recv(halo1)
    wz_lo = 0.5 * (eps[first, :] + zlo[X:2 * X, :])
    wz_hi = 0.5 * (eps[last, :] + zhi[X:2 * X, :])
    num[first, :] = num[first, :] - wz_lo * (pot[first, :] - zlo[0:X, :])
    num[last, :] = num[last, :] - wz_hi * (pot[last, :] - zhi[0:X, :])
    dia[first, :] = dia[first, :] + wz_lo
    dia[last, :] = dia[last, :] + wz_hi
    for k, (own, halo) in enumerate(((xs_lo, xlo), (xs_hi, xhi))):
        w = 0.5 * (own[Z:2 * Z, :] + halo[Z:2 * Z, :])
        fx[2 * k * Z:(2 * k + 1) * Z, :] = w * (own[0:Z, :] - halo[0:Z, :])
        fx[(2 * k + 1) * Z:(2 * k + 2) * Z, :] = w
    even = lane % 2 == 0
    own_y = pltpu.roll(ys[...], 127, 1)
    halo_y = jnp.where(even, ylo[...], pltpu.roll(yhi[...], 126, 1))
    wy_end = 0.5 * (pltpu.roll(own_y, 64, 1) + pltpu.roll(halo_y, 64, 1))
    fy_end = wy_end * (own_y - halo_y)

    def at_ends(value):
        return jnp.concatenate([jnp.where(lane == 0, value, 0.0), jnp.where(lane == 127, value, 0.0)], axis=1)

    row8 = lax.broadcasted_iota(jnp.int32, (X // 2, Y), 0)

    def at_rows(low, high):
        return jnp.concatenate([jnp.where(row8 == 0, low, 0.0), jnp.where(row8 == X // 2 - 1, high, 0.0)], axis=0)

    def sweep(zc, acc):
        total = jnp.zeros((X, Y), F32)
        for dz in range(4):
            z = zc * 4 + dz
            shift = lax.rem(128 - 2 * z, 128)
            f = at_ends(pltpu.roll(fy_end, shift, 1))
            w = at_ends(pltpu.roll(wy_end, shift, 1))
            f = f + at_rows(fx[pl.ds(z, 1), :], fx[pl.ds(2 * Z + z, 1), :])
            w = w + at_rows(fx[pl.ds(Z + z, 1), :], fx[pl.ds(3 * Z + z, 1), :])
            d = dia[slab(z), :] + w
            total = total + d
            sw = pot[slab(z), :] + OMEGA * (num[slab(z), :] - f) / d
            swp[slab(z), :] = sw
            xs_lo2[pl.ds(z, 1), :] = sw[0:1, :]
            xs_hi2[pl.ds(z, 1), :] = sw[X - 1:X, :]
            acc = jnp.where(pair == z, pltpu.roll(ends(sw), 2 * z + 1, 1), acc)
        zsd[slab(zc), :] = total
        return acc
    ys2 = lax.fori_loop(0, CZ, sweep, jnp.zeros((X, 128), F32), unroll=4)

    def residual_local(zc, fz_prev):
        total = jnp.zeros((X, Y), F32)
        for dz in range(4):
            z = zc * 4 + dz
            v, e = swp[slab(z), :], eps[slab(z), :]
            up_z = jnp.minimum(z + 1, Z - 1)
            inside = jnp.where(z < Z - 1, 0.5, 0.0).astype(F32)
            fz = inside * (e + eps[slab(up_z), :]) * (v - swp[slab(up_z), :])
            fxl = wxs[slab(z), :] * (v - pltpu.roll(v, X - 1, 0))
            fyl = wys[slab(z), :] * (v - pltpu.roll(v, Y - 1, 1))
            flux = (fz - fz_prev) + (fxl - pltpu.roll(fxl, 1, 0)) + (fyl - pltpu.roll(fyl, 1, 1))
            total = total + (CHARGE_SCALE * chg[slab(z), :] - flux - scr[slab(z), :] * (0.5 * (jnp.exp(v) - jnp.exp(-v))))
            fz_prev = fz
        zsr[slab(zc), :] = total
        return fz_prev
    lax.fori_loop(0, CZ, residual_local, zero, unroll=2)

    merge = jnp.where(lax.broadcasted_iota(jnp.int32, (Y, 128), 0) // 4 == lax.broadcasted_iota(jnp.int32, (Y, 128), 1) % A, 1.0, 0.0).astype(BF16)

    def coarse_rows(ref):
        groups = []
        for xc in range(CX):
            rows = []
            for zc in range(CZ):
                base = zc * X + 4 * xc
                block = ref[zc * X + (xc // 2) * 8:zc * X + (xc // 2) * 8 + 8, :]
                rows.append(jnp.sum(block[(xc % 2) * 4:(xc % 2) * 4 + 4, :], axis=0, keepdims=True))
            groups.append(jnp.concatenate(rows, axis=0))
        return groups

    def merged(groups):
        high, low = split2(jnp.concatenate(groups, axis=0))
        both = jnp.dot(jnp.concatenate([high, low], axis=0), merge, preferred_element_type=F32)
        return (both[0:high.shape[0], :] + both[high.shape[0]:, :]) * (1.0 / 64.0)

    z_lo, z_hi = wz_lo * swp[first, :], wz_hi * swp[last, :]
    zsr[0:X, :] = zsr[0:X, :] - z_lo
    zsr[(CZ - 1) * X:CZ * X, :] = zsr[(CZ - 1) * X:CZ * X, :] - z_hi
    f = wy_end * pltpu.roll(ys2, 127, 1)
    f = f + pltpu.roll(f, 126, 1)
    f = f + pltpu.roll(f, 124, 1)
    for zc in range(CZ):
        zsr[zc * X:(zc + 1) * X, :] = zsr[zc * X:(zc + 1) * X, :] - at_ends(pltpu.roll(f, (128 - 8 * zc) % 128, 1))
    groups = coarse_rows(zsr)

    def sum_rows(value):
        return jnp.concatenate([jnp.sum(value[i:i + 4, :], axis=0, keepdims=True) for i in range(0, value.shape[0], 4)], axis=0)

    x_lo, x_hi = sum_rows(fx[Z:2 * Z, :] * xs_lo2[...]), sum_rows(fx[3 * Z:4 * Z, :] * xs_hi2[...])
    groups[0] = groups[0] - x_lo
    groups[-1] = groups[-1] - x_hi
    z_sums = jnp.concatenate([sum_rows(z_lo), sum_rows(z_hi)], axis=0)
    both = merged(groups + [x_lo, x_hi, z_sums, jnp.zeros_like(z_sums)])
    ROWS = NC + 2 * CZ
    mine[...] = both[0:ROWS, :]
    zsend_lo[0:CX, :] = both[ROWS:ROWS + CX, :]
    zsend_hi[0:CX, :] = both[ROWS + CX:ROWS + 2 * CX, :]
    ysend[0:CX, :] = sum_rows(f) * (1.0 / 64.0)
    for ref in (zsend_lo, zsend_hi, ysend):
        ref[CX:8, :] = jnp.zeros((8 - CX, 128), F32)

    def to_peer(src, dst, lane_of_sem, d, axis, step):
        return pltpu.make_async_remote_copy(
            src_ref=src, dst_ref=dst, send_sem=gsend.at[lane_of_sem * n + d], recv_sem=grecv.at[lane_of_sem * n + d],
            device_id=peer(d, axis, step), device_id_type=MESH)

    at_mine = pl.ds(pl.multiple_of(ids[0] * ROWS, 16), ROWS)
    at_eight = pl.ds(pl.multiple_of(ids[0] * 8, 8), 8)
    shares = []
    for kind, (axis, step, src, dst) in enumerate(((1, 1, ysend, yin_lo), (1, -1, ysend, yin_hi), (2, 1, zsend_hi, zin_lo), (2, -1, zsend_lo, zin_hi))):
        shares.append((axis, step == 1, [to_peer(src, dst.at[at_eight, :], kind + 1, d, axis, step) for d in range(n)]))
    gathers = [to_peer(mine, parts.at[at_mine, :], 0, d, 0, 0) for d in range(1, n)]
    for copy in gathers:
        copy.start()
    for axis, upward, copies in shares:
        @pl.when(high_ok(axis) if upward else low_ok(axis))
        def _(copies=copies):
            for copy in copies:
                copy.start()
    parts[at_mine, :] = both[0:ROWS, :]

    coarse_diag = merged(coarse_rows(zsd))

    for copy in gathers:
        copy.wait_recv()
    for axis, upward, copies in shares:
        @pl.when(low_ok(axis) if upward else high_ok(axis))
        def _(copies=copies):
            for copy in copies:
                copy.wait_recv()
    sub8 = lax.broadcasted_iota(jnp.int32, (CZ, 128), 0)
    lane8 = lax.broadcasted_iota(jnp.int32, (CZ, 128), 1)
    low_lane, high_lane = lane8 == 8 * sub8, lane8 == (8 * sub8 + 127) % 128
    first_cell, last_cell = lane8 % A == 0, lane8 % A == A - 1
    for g in range(n):
        for xc in range(CX):
            b = parts[g * ROWS + xc * CZ:g * ROWS + (xc + 1) * CZ, :]
            if xc == 0 and g > 0:
                b = b + parts[(g - 1) * ROWS + NC + CZ:g * ROWS, :]
            if xc == CX - 1 and g < n - 1:
                b = b + parts[(g + 1) * ROWS + NC:(g + 1) * ROWS + NC + CZ, :]
            here = slice(g * 8 + xc, g * 8 + xc + 1)
            b = b + jnp.where(sub8 == 0, zin_lo[here, :], 0.0) + jnp.where(sub8 == CZ - 1, zin_hi[here, :], 0.0)
            from_low = jnp.sum(jnp.where(high_lane, yin_lo[here, :], 0.0), axis=1, keepdims=True)
            from_high = jnp.sum(jnp.where(low_lane, yin_hi[here, :], 0.0), axis=1, keepdims=True)
            b = b + jnp.where(first_cell, from_low, 0.0) + jnp.where(last_cell, from_high, 0.0)
            col[g * NC + xc * CZ:g * NC + (xc + 1) * CZ, :] = b
    coarse_resid = col[pl.ds(pl.multiple_of(ids[0] * NC, NC), NC), :]

    left = lax.broadcasted_iota(jnp.int32, (CZ, 128), 1) < A
    picked = jnp.dot(choose[...].astype(BF16), jnp.concatenate(split2(col[...]), axis=1), preferred_element_type=F32)
    zrow = lax.broadcasted_iota(jnp.int32, (CZ, 128), 0)
    rows = []
    for xc in range(CX):
        p0, p1 = picked[xc * CZ:(xc + 1) * CZ, :], picked[(CX + xc) * CZ:(CX + xc + 1) * CZ, :]
        high, low = [jnp.where(left, p0[:, i:i + 128], p1[:, i:i + 128]) for i in (0, 128)]
        lhs = jnp.concatenate([jnp.concatenate([high, high], axis=1),
                               jnp.concatenate([low, jnp.zeros_like(low)], axis=1)], axis=0).astype(BF16)
        prod = lax.dot_general(lhs, weights[xc], (((1,), (1,)), ((), ())), preferred_element_type=F32)
        prod = prod[0:CZ, :] + prod[CZ:2 * CZ, :]
        mine_only = jnp.zeros((CZ, 128), F32)
        for i in range(CZ // 2):
            mine_only = jnp.where(zrow // 2 == i, prod[:, i * 128:(i + 1) * 128], mine_only)
        rows.append(jnp.where(left == (zrow % 2 == 0), mine_only, pltpu.roll(mine_only, A, 1)))
    coupled = jnp.concatenate(rows, axis=0)

    correction = COARSE_SCALE * (coarse_resid + coupled) / coarse_diag
    cor[...] = correction
    high, low = split2(jnp.where(lax.broadcasted_iota(jnp.int32, (NC, 128), 1) < A, correction, 0.0))
    both = lax.dot_general(jnp.concatenate([high, low], axis=0), merge, (((1,), (1,)), ((), ())), preferred_element_type=F32)
    spread[...] = both[0:NC, :] + both[NC:2 * NC, :]
    wait_send(halo1)
    for copy in gathers:
        copy.wait_send()
    for axis, upward, copies in shares:
        @pl.when(high_ok(axis) if upward else low_ok(axis))
        def _(copies=copies):
            for copy in copies:
                copy.wait_send()


def finish(Z, X, Y, A, swp, spread, cor, out, corr, stage, small, sem):
    CZ, CX = Z // 4, X // 4
    for xc in range(CX):
        small[:, xc, 0, :] = cor[xc * CZ:(xc + 1) * CZ, 0:A]
    copies = [pltpu.make_async_copy(small, corr, sem.at[CZ])]
    copies[0].start()
    quarter = lax.broadcasted_iota(jnp.int32, (X, Y), 0) // 4
    for zc in range(CZ):
        add = jnp.zeros((X, Y), F32)
        for xc in range(CX):
            add = jnp.where(quarter == xc, spread[xc * CZ + zc:xc * CZ + zc + 1, :], add)
        for z in range(zc * 4, zc * 4 + 4):
            stage[z * X:(z + 1) * X, :] = swp[z * X:(z + 1) * X, :] + add
        rows = pl.ds(zc * 4 * X, 4 * X)
        copy = pltpu.make_async_copy(stage.at[rows, :], out.at[rows, :], sem.at[zc])
        copy.start()
        copies.append(copy)
    for copy in copies:
        copy.wait()


def solution(mesh):
    counts = (mesh.shape["gx"], mesh.shape["gy"], mesh.shape["gz"])

    def per_device(potential, charge, permittivity, labels, pattern, blocks):
        Z, X, Y = potential.shape
        A = blocks.shape[-1]
        CZ, CX = Z // 4, X // 4
        NC = CZ * CX
        flat = (Z * X, Y)
        whole = pltpu.VMEM(flat, F32)
        any_spec = pl.BlockSpec(memory_space=pltpu.HBM)
        vmem = pl.BlockSpec(memory_space=pltpu.VMEM)
        n = counts[0]

        swept, spread, cor = pl.pallas_call(
            functools.partial(kernel, counts, Z, X, Y, A),
            out_shape=(whole, pltpu.VMEM((NC, Y), F32), pltpu.VMEM((NC, 128), F32)),
            in_specs=[any_spec] * 6,
            out_specs=(vmem, vmem, vmem),
            scratch_shapes=[
                pltpu.VMEM((CX, 1, 2, CZ), jnp.int32), whole, whole, whole, pltpu.VMEM(flat, jnp.int32), pltpu.VMEM((2 * NC, A, A), F32),
                whole, whole, whole, whole, whole,
                *[pltpu.VMEM((2 * X, Y), F32)] * 2, *[pltpu.VMEM((2 * Z, Y), F32)] * 2, *[pltpu.VMEM((X, 128), F32)] * 2,
                *[pltpu.VMEM((2 * Z, Y), F32)] * 2, pltpu.VMEM((X, 128), F32),
                *[pltpu.VMEM((Z, Y), F32)] * 2,
                pltpu.VMEM((4 * Z, Y), F32), pltpu.VMEM((CZ * X, Y), F32), pltpu.VMEM((CZ * X, Y), F32),
                pltpu.VMEM((CX, CZ * A, 4 * A), BF16), pltpu.VMEM((NC + 2 * CZ, 128), F32), *[pltpu.VMEM((8, 128), F32)] * 3,
                pltpu.VMEM((n * NC, 128), F32), pltpu.VMEM((n * (NC + 2 * CZ), 128), F32), *[pltpu.VMEM((n * 8, 128), F32)] * 4,
                pltpu.VMEM((2 * NC, n * NC), F32),
                pltpu.SemaphoreType.DMA((6,)), pltpu.SemaphoreType.DMA((8,)), pltpu.SemaphoreType.DMA((8,)),
                pltpu.SemaphoreType.DMA((5 * n,)), pltpu.SemaphoreType.DMA((5 * n,)),
            ],
            compiler_params=pltpu.CompilerParams(
                collective_id=0, has_side_effects=True, vmem_limit_bytes=32 * 1024 * 1024),
        )(*[pltpu.with_memory_space_constraint(x, pltpu.HBM) for x in (
            jnp.transpose(pattern, (1, 2, 3, 0)), potential.reshape(flat), charge.reshape(flat), permittivity.reshape(flat),
            labels.reshape(flat), blocks.reshape(2 * NC, A, A))])
        out, corr = pl.pallas_call(
            functools.partial(finish, Z, X, Y, A),
            out_shape=(jax.ShapeDtypeStruct(flat, F32), jax.ShapeDtypeStruct((CZ, CX, 1, A), F32)),
            in_specs=[vmem] * 3,
            out_specs=(any_spec, any_spec),
            scratch_shapes=[whole, pltpu.VMEM((CZ, CX, 1, A), F32), pltpu.SemaphoreType.DMA((CZ + 1,))],
            compiler_params=pltpu.CompilerParams(vmem_limit_bytes=32 * 1024 * 1024),
        )(swept, spread, cor)
        return out.reshape(Z, X, Y), corr

    return jax.shard_map(
        per_device,
        mesh=mesh,
        in_specs=(
            P("gz", "gx", "gy"),
            P("gz", "gx", "gy"),
            P("gz", "gx", "gy"),
            P("gz", "gx", "gy"),
            P("gz", "gx", "gy", None),
            P("gz", "gx", "gy", None, None, None),
        ),
        out_specs=(P("gz", "gx", "gy"), P("gz", "gx", "gy", None)),
        check_vma=False,
    )
```

```python
import functools

import jax
import jax.numpy as jnp
from jax import lax
from jax.experimental import pallas as pl
from jax.experimental.pallas import tpu as pltpu
from jax.sharding import PartitionSpec as P

OMEGA = 0.8
CHARGE_SCALE = 40.0
COARSE_SCALE = 4.0
MESH = pl.DeviceIdType.MESH
F32 = jnp.float32
BF16 = jnp.bfloat16


def split2(value):
    high = value.astype(BF16)
    return high, (value - high.astype(F32)).astype(BF16)


def kernel(counts, Z, X, Y, A, pat_h, pot_h, chg_h, eps_h, lab_h, blk_h, swp, spread, cor,
           pat, pot, chg, eps, lab, blk, num, dia, scr, wxs, wys,
           zlo, zhi, xlo, xhi, ylo, yhi, xs_lo, xs_hi, ys,
           xs_lo2, xs_hi2, fx, zsr, zsd, weights, mine, zsend_lo, zsend_hi, ysend, col, parts, zin_lo, zin_hi, yin_lo, yin_hi, choose,
           in_sem, send_sem, recv_sem, gsend, grecv):
    ids = [lax.axis_index(name) for name in ("gx", "gy", "gz")]
    CZ, CX = Z // 4, X // 4
    NC = CZ * CX
    half = Y // 2

    loads = [pltpu.make_async_copy(s, d, in_sem.at[i])
             for i, (s, d) in enumerate(((pot_h, pot), (eps_h, eps), (chg_h, chg), (lab_h, lab), (pat_h, pat), (blk_h, blk)))]
    for load in loads[:2]:
        load.start()

    def at(axis, index):
        return tuple(index if a == axis else ids[a] for a in range(3))

    def low_ok(axis):
        return ids[axis] > 0

    def high_ok(axis):
        return ids[axis] < counts[axis] - 1

    barrier = pltpu.get_barrier_semaphore()
    n = counts[0]

    def peer(d, axis=0, step=0):
        target = list(ids)
        if axis:
            target[axis] = jnp.clip(ids[axis] + step, 0, counts[axis] - 1)
        target[0] = lax.rem(ids[0] + d, n)
        return tuple(target)

    for d in range(1, n):
        pl.semaphore_signal(barrier, inc=1, device_id=peer(d), device_id_type=MESH)
    expected = n - 1
    for axis in (1, 2):
        for ok, step in ((low_ok(axis), -1), (high_ok(axis), 1)):
            @pl.when(ok)
            def _(axis=axis, step=step):
                pl.semaphore_signal(barrier, inc=1, device_id=peer(0, axis, step), device_id_type=MESH)
            expected = expected + ok.astype(jnp.int32)

    for axis, lo_bufs, hi_bufs in ((2, (zlo, zin_lo), (zhi, zin_hi)), (0, (xlo,), (xhi,)), (1, (ylo, yin_lo), (yhi, yin_hi))):
        @pl.when(jnp.logical_not(low_ok(axis)))
        def _(bufs=lo_bufs):
            for b in bufs:
                b[...] = jnp.zeros_like(b)

        @pl.when(jnp.logical_not(high_ok(axis)))
        def _(bufs=hi_bufs):
            for b in bufs:
                b[...] = jnp.zeros_like(b)

    def up(axis, src, dst, sem):
        return (axis, True, pltpu.make_async_remote_copy(
            src_ref=src, dst_ref=dst, send_sem=send_sem.at[sem], recv_sem=recv_sem.at[sem],
            device_id=at(axis, jnp.minimum(ids[axis] + 1, counts[axis] - 1)), device_id_type=MESH))

    def down(axis, src, dst, sem):
        return (axis, False, pltpu.make_async_remote_copy(
            src_ref=src, dst_ref=dst, send_sem=send_sem.at[sem], recv_sem=recv_sem.at[sem],
            device_id=at(axis, jnp.maximum(ids[axis] - 1, 0)), device_id_type=MESH))

    def start(messages):
        for axis, upward, copy in messages:
            @pl.when(high_ok(axis) if upward else low_ok(axis))
            def _(copy=copy):
                copy.start()

    def wait_recv(messages):
        for axis, upward, copy in messages:
            @pl.when(low_ok(axis) if upward else high_ok(axis))
            def _(copy=copy):
                copy.wait_recv()

    def wait_send(messages):
        for axis, upward, copy in messages:
            @pl.when(high_ok(axis) if upward else low_ok(axis))
            def _(copy=copy):
                copy.wait_send()

    def slab(z):
        return pl.ds(pl.multiple_of(z * X, X), X)

    lane = lax.broadcasted_iota(jnp.int32, (X, 128), 1)
    pair = lane // 2
    row = lax.broadcasted_iota(jnp.int32, (X, Y), 0)
    ylane = lax.broadcasted_iota(jnp.int32, (X, Y), 1)

    def ends(value):
        return jnp.where(lane == 127, value[:, half:][:, -128:], value[:, :128])

    loads[0].wait()
    loads[1].wait()
    for load in loads[2:]:
        load.start()
    for z in range(Z):
        for k, field in enumerate((pot, eps)):
            xs_lo[k * Z + z:k * Z + z + 1, :] = field[z * X:z * X + 1, :]
            xs_hi[k * Z + z:k * Z + z + 1, :] = field[z * X + X - 1:z * X + X, :]
    pl.semaphore_wait(barrier, expected)
    first = pl.ds(0, X)
    last = pl.ds((Z - 1) * X, X)
    halo1 = [
        up(0, xs_hi, xlo, 0), down(0, xs_lo, xhi, 1),
        up(2, pot.at[last, :], zlo.at[pl.ds(0, X), :], 4), up(2, eps.at[last, :], zlo.at[pl.ds(X, X), :], 5),
        down(2, pot.at[first, :], zhi.at[pl.ds(0, X), :], 6), down(2, eps.at[first, :], zhi.at[pl.ds(X, X), :], 7),
        up(1, ys, ylo, 2), down(1, ys, yhi, 3),
    ]
    start(halo1[:6])
    def pack1(z, acc):
        acc = jnp.where(pair == z, pltpu.roll(ends(pot[slab(z), :]), 2 * z + 1, 1), acc)
        return jnp.where(pair == z + 32, pltpu.roll(ends(eps[slab(z), :]), 2 * z + 65, 1), acc)
    ys[...] = lax.fori_loop(0, Z, pack1, jnp.zeros((X, 128), F32), unroll=8)
    start(halo1[6:])
    loads[2].wait()
    loads[3].wait()

    not_top = row < X - 1
    not_end = ylane < Y - 1

    def sweep_local(z, carry):
        fz_prev, wz_prev = carry
        v, e = pot[slab(z), :], eps[slab(z), :]
        up_z = jnp.minimum(z + 1, Z - 1)
        inside = jnp.where(z < Z - 1, 0.5, 0.0).astype(F32)
        wz = inside * (e + eps[slab(up_z), :])
        fz = wz * (v - pot[slab(up_z), :])
        wx = jnp.where(not_top, 0.5 * (e + pltpu.roll(e, X - 1, 0)), 0.0)
        fxl = wx * (v - pltpu.roll(v, X - 1, 0))
        wy = jnp.where(not_end, 0.5 * (e + pltpu.roll(e, Y - 1, 1)), 0.0)
        fyl = wy * (v - pltpu.roll(v, Y - 1, 1))
        flux = (fz - fz_prev) + (fxl - pltpu.roll(fxl, 1, 0)) + (fyl - pltpu.roll(fyl, 1, 1))
        faces = (wz + wz_prev) + (wx + pltpu.roll(wx, 1, 0)) + (wy + pltpu.roll(wy, 1, 1))
        labels = lab[slab(z), :]
        s = e * jnp.where(labels == 1, 0.05, jnp.where(labels == 2, 0.2, 0.0))
        ep, em = jnp.exp(v), jnp.exp(-v)
        wxs[slab(z), :] = wx
        wys[slab(z), :] = wy
        scr[slab(z), :] = s
        num[slab(z), :] = CHARGE_SCALE * chg[slab(z), :] - flux - s * (0.5 * (ep - em))
        dia[slab(z), :] = faces + s * (0.5 * (ep + em))
        return fz, wz
    zero = jnp.zeros((X, Y), F32)
    lax.fori_loop(0, Z, sweep_local, (zero, zero), unroll=8)

    loads[5].wait()
    def split_blocks(zc, c):
        for xc in range(CX):
            at_block = (zc * CX + xc) * 2
            both = jnp.concatenate([blk[at_block], blk[at_block + 1]], axis=1)
            high, low = split2(both)
            here = pl.ds(pl.multiple_of(zc * A, A), A)
            weights[xc, here, 0:2 * A] = high
            weights[xc, here, 2 * A:4 * A] = low
        return c
    lax.fori_loop(0, CZ, split_blocks, 0)

    loads[4].wait()
    diagonal = lax.broadcasted_iota(jnp.int32, (CZ, CZ), 0) == lax.broadcasted_iota(jnp.int32, (CZ, CZ), 1)
    names = lax.broadcasted_iota(jnp.int32, (CZ, n * NC), 1).astype(F32)
    for k in range(2):
        for xc in range(CX):
            wanted = jnp.sum(jnp.where(diagonal, pat[xc, 0, k:k + 1, :].astype(F32), 0.0), axis=1, keepdims=True)
            at_row = (k * CX + xc) * CZ
            choose[at_row:at_row + CZ, :] = jnp.where(names == wanted, 1.0, 0.0)

    wait_recv(halo1)
    wz_lo = 0.5 * (eps[first, :] + zlo[X:2 * X, :])
    wz_hi = 0.5 * (eps[last, :] + zhi[X:2 * X, :])
    num[first, :] = num[first, :] - wz_lo * (pot[first, :] - zlo[0:X, :])
    num[last, :] = num[last, :] - wz_hi * (pot[last, :] - zhi[0:X, :])
    dia[first, :] = dia[first, :] + wz_lo
    dia[last, :] = dia[last, :] + wz_hi
    for k, (own, halo) in enumerate(((xs_lo, xlo), (xs_hi, xhi))):
        w = 0.5 * (own[Z:2 * Z, :] + halo[Z:2 * Z, :])
        fx[2 * k * Z:(2 * k + 1) * Z, :] = w * (own[0:Z, :] - halo[0:Z, :])
        fx[(2 * k + 1) * Z:(2 * k + 2) * Z, :] = w
    even = lane % 2 == 0
    own_y = pltpu.roll(ys[...], 127, 1)
    halo_y = jnp.where(even, ylo[...], pltpu.roll(yhi[...], 126, 1))
    wy_end = 0.5 * (pltpu.roll(own_y, 64, 1) + pltpu.roll(halo_y, 64, 1))
    fy_end = wy_end * (own_y - halo_y)

    def at_ends(value):
        return jnp.concatenate([jnp.where(lane == 0, value, 0.0), jnp.where(lane == 127, value, 0.0)], axis=1)

    row8 = lax.broadcasted_iota(jnp.int32, (X // 2, Y), 0)

    def at_rows(low, high):
        return jnp.concatenate([jnp.where(row8 == 0, low, 0.0), jnp.where(row8 == X // 2 - 1, high, 0.0)], axis=0)

    def sweep(zc, acc):
        total = jnp.zeros((X, Y), F32)
        for dz in range(4):
            z = zc * 4 + dz
            shift = lax.rem(128 - 2 * z, 128)
            f = at_ends(pltpu.roll(fy_end, shift, 1))
            w = at_ends(pltpu.roll(wy_end, shift, 1))
            f = f + at_rows(fx[pl.ds(z, 1), :], fx[pl.ds(2 * Z + z, 1), :])
            w = w + at_rows(fx[pl.ds(Z + z, 1), :], fx[pl.ds(3 * Z + z, 1), :])
            d = dia[slab(z), :] + w
            total = total + d
            sw = pot[slab(z), :] + OMEGA * (num[slab(z), :] - f) / d
            swp[slab(z), :] = sw
            xs_lo2[pl.ds(z, 1), :] = sw[0:1, :]
            xs_hi2[pl.ds(z, 1), :] = sw[X - 1:X, :]
            acc = jnp.where(pair == z, pltpu.roll(ends(sw), 2 * z + 1, 1), acc)
        zsd[slab(zc), :] = total
        return acc
    ys2 = lax.fori_loop(0, CZ, sweep, jnp.zeros((X, 128), F32), unroll=8)

    def residual_local(zc, fz_prev):
        total = jnp.zeros((X, Y), F32)
        for dz in range(4):
            z = zc * 4 + dz
            v, e = swp[slab(z), :], eps[slab(z), :]
            up_z = jnp.minimum(z + 1, Z - 1)
            inside = jnp.where(z < Z - 1, 0.5, 0.0).astype(F32)
            fz = inside * (e + eps[slab(up_z), :]) * (v - swp[slab(up_z), :])
            fxl = wxs[slab(z), :] * (v - pltpu.roll(v, X - 1, 0))
            fyl = wys[slab(z), :] * (v - pltpu.roll(v, Y - 1, 1))
            flux = (fz - fz_prev) + (fxl - pltpu.roll(fxl, 1, 0)) + (fyl - pltpu.roll(fyl, 1, 1))
            total = total + (CHARGE_SCALE * chg[slab(z), :] - flux - scr[slab(z), :] * (0.5 * (jnp.exp(v) - jnp.exp(-v))))
            fz_prev = fz
        zsr[slab(zc), :] = total
        return fz_prev
    lax.fori_loop(0, CZ, residual_local, zero, unroll=4)

    merge = jnp.where(lax.broadcasted_iota(jnp.int32, (Y, 128), 0) // 4 == lax.broadcasted_iota(jnp.int32, (Y, 128), 1) % A, 1.0, 0.0).astype(BF16)

    def coarse_rows(ref):
        groups = []
        for xc in range(CX):
            rows = []
            for zc in range(CZ):
                base = zc * X + 4 * xc
                block = ref[zc * X + (xc // 2) * 8:zc * X + (xc // 2) * 8 + 8, :]
                rows.append(jnp.sum(block[(xc % 2) * 4:(xc % 2) * 4 + 4, :], axis=0, keepdims=True))
            groups.append(jnp.concatenate(rows, axis=0))
        return groups

    def merged(groups):
        high, low = split2(jnp.concatenate(groups, axis=0))
        both = jnp.dot(jnp.concatenate([high, low], axis=0), merge, preferred_element_type=F32)
        return (both[0:high.shape[0], :] + both[high.shape[0]:, :]) * (1.0 / 64.0)

    z_lo, z_hi = wz_lo * swp[first, :], wz_hi * swp[last, :]
    zsr[0:X, :] = zsr[0:X, :] - z_lo
    zsr[(CZ - 1) * X:CZ * X, :] = zsr[(CZ - 1) * X:CZ * X, :] - z_hi
    f = wy_end * pltpu.roll(ys2, 127, 1)
    f = f + pltpu.roll(f, 126, 1)
    f = f + pltpu.roll(f, 124, 1)
    for zc in range(CZ):
        zsr[zc * X:(zc + 1) * X, :] = zsr[zc * X:(zc + 1) * X, :] - at_ends(pltpu.roll(f, (128 - 8 * zc) % 128, 1))
    groups = coarse_rows(zsr)

    def sum_rows(value):
        return jnp.concatenate([jnp.sum(value[i:i + 4, :], axis=0, keepdims=True) for i in range(0, value.shape[0], 4)], axis=0)

    x_lo, x_hi = sum_rows(fx[Z:2 * Z, :] * xs_lo2[...]), sum_rows(fx[3 * Z:4 * Z, :] * xs_hi2[...])
    groups[0] = groups[0] - x_lo
    groups[-1] = groups[-1] - x_hi
    z_sums = jnp.concatenate([sum_rows(z_lo), sum_rows(z_hi)], axis=0)
    both = merged(groups + [x_lo, x_hi, z_sums, jnp.zeros_like(z_sums)])
    ROWS = NC + 2 * CZ
    mine[...] = both[0:ROWS, :]
    zsend_lo[0:CX, :] = both[ROWS:ROWS + CX, :]
    zsend_hi[0:CX, :] = both[ROWS + CX:ROWS + 2 * CX, :]
    ysend[0:CX, :] = sum_rows(f) * (1.0 / 64.0)
    for ref in (zsend_lo, zsend_hi, ysend):
        ref[CX:8, :] = jnp.zeros((8 - CX, 128), F32)

    def to_peer(src, dst, lane_of_sem, d, axis, step):
        return pltpu.make_async_remote_copy(
            src_ref=src, dst_ref=dst, send_sem=gsend.at[lane_of_sem * n + d], recv_sem=grecv.at[lane_of_sem * n + d],
            device_id=peer(d, axis, step), device_id_type=MESH)

    at_mine = pl.ds(pl.multiple_of(ids[0] * ROWS, 16), ROWS)
    at_eight = pl.ds(pl.multiple_of(ids[0] * 8, 8), 8)
    shares = []
    for kind, (axis, step, src, dst) in enumerate(((1, 1, ysend, yin_lo), (1, -1, ysend, yin_hi), (2, 1, zsend_hi, zin_lo), (2, -1, zsend_lo, zin_hi))):
        shares.append((axis, step == 1, [to_peer(src, dst.at[at_eight, :], kind + 1, d, axis, step) for d in range(n)]))
    gathers = [to_peer(mine, parts.at[at_mine, :], 0, d, 0, 0) for d in range(1, n)]
    for copy in gathers:
        copy.start()
    for axis, upward, copies in shares:
        @pl.when(high_ok(axis) if upward else low_ok(axis))
        def _(copies=copies):
            for copy in copies:
                copy.start()
    parts[at_mine, :] = both[0:ROWS, :]

    coarse_diag = merged(coarse_rows(zsd))

    for copy in gathers:
        copy.wait_recv()
    for axis, upward, copies in shares:
        @pl.when(low_ok(axis) if upward else high_ok(axis))
        def _(copies=copies):
            for copy in copies:
                copy.wait_recv()
    sub8 = lax.broadcasted_iota(jnp.int32, (CZ, 128), 0)
    lane8 = lax.broadcasted_iota(jnp.int32, (CZ, 128), 1)
    low_lane, high_lane = lane8 == 8 * sub8, lane8 == (8 * sub8 + 127) % 128
    first_cell, last_cell = lane8 % A == 0, lane8 % A == A - 1
    for g in range(n):
        for xc in range(CX):
            b = parts[g * ROWS + xc * CZ:g * ROWS + (xc + 1) * CZ, :]
            if xc == 0 and g > 0:
                b = b + parts[(g - 1) * ROWS + NC + CZ:g * ROWS, :]
            if xc == CX - 1 and g < n - 1:
                b = b + parts[(g + 1) * ROWS + NC:(g + 1) * ROWS + NC + CZ, :]
            here = slice(g * 8 + xc, g * 8 + xc + 1)
            b = b + jnp.where(sub8 == 0, zin_lo[here, :], 0.0) + jnp.where(sub8 == CZ - 1, zin_hi[here, :], 0.0)
            from_low = jnp.sum(jnp.where(high_lane, yin_lo[here, :], 0.0), axis=1, keepdims=True)
            from_high = jnp.sum(jnp.where(low_lane, yin_hi[here, :], 0.0), axis=1, keepdims=True)
            b = b + jnp.where(first_cell, from_low, 0.0) + jnp.where(last_cell, from_high, 0.0)
            col[g * NC + xc * CZ:g * NC + (xc + 1) * CZ, :] = b
    coarse_resid = col[pl.ds(pl.multiple_of(ids[0] * NC, NC), NC), :]

    left = lax.broadcasted_iota(jnp.int32, (CZ, 128), 1) < A
    picked = jnp.dot(choose[...].astype(BF16), jnp.concatenate(split2(col[...]), axis=1), preferred_element_type=F32)
    zrow = lax.broadcasted_iota(jnp.int32, (CZ, 128), 0)
    rows = []
    for xc in range(CX):
        p0, p1 = picked[xc * CZ:(xc + 1) * CZ, :], picked[(CX + xc) * CZ:(CX + xc + 1) * CZ, :]
        high, low = [jnp.where(left, p0[:, i:i + 128], p1[:, i:i + 128]) for i in (0, 128)]
        lhs = jnp.concatenate([jnp.concatenate([high, high], axis=1),
                               jnp.concatenate([low, jnp.zeros_like(low)], axis=1)], axis=0).astype(BF16)
        prod = lax.dot_general(lhs, weights[xc], (((1,), (1,)), ((), ())), preferred_element_type=F32)
        prod = prod[0:CZ, :] + prod[CZ:2 * CZ, :]
        mine_only = jnp.zeros((CZ, 128), F32)
        for i in range(CZ // 2):
            mine_only = jnp.where(zrow // 2 == i, prod[:, i * 128:(i + 1) * 128], mine_only)
        rows.append(jnp.where(left == (zrow % 2 == 0), mine_only, pltpu.roll(mine_only, A, 1)))
    coupled = jnp.concatenate(rows, axis=0)

    correction = COARSE_SCALE * (coarse_resid + coupled) / coarse_diag
    cor[...] = correction
    high, low = split2(jnp.where(lax.broadcasted_iota(jnp.int32, (NC, 128), 1) < A, correction, 0.0))
    both = lax.dot_general(jnp.concatenate([high, low], axis=0), merge, (((1,), (1,)), ((), ())), preferred_element_type=F32)
    spread[...] = both[0:NC, :] + both[NC:2 * NC, :]
    wait_send(halo1)
    for copy in gathers:
        copy.wait_send()
    for axis, upward, copies in shares:
        @pl.when(high_ok(axis) if upward else low_ok(axis))
        def _(copies=copies):
            for copy in copies:
                copy.wait_send()


def finish(Z, X, Y, A, swp, spread, cor, out, corr, stage, small, sem):
    CZ, CX = Z // 4, X // 4
    for xc in range(CX):
        small[:, xc, 0, :] = cor[xc * CZ:(xc + 1) * CZ, 0:A]
    copies = [pltpu.make_async_copy(small, corr, sem.at[CZ])]
    copies[0].start()
    quarter = lax.broadcasted_iota(jnp.int32, (X, Y), 0) // 4
    for zc in range(CZ):
        add = jnp.zeros((X, Y), F32)
        for xc in range(CX):
            add = jnp.where(quarter == xc, spread[xc * CZ + zc:xc * CZ + zc + 1, :], add)
        for z in range(zc * 4, zc * 4 + 4):
            stage[z * X:(z + 1) * X, :] = swp[z * X:(z + 1) * X, :] + add
        rows = pl.ds(zc * 4 * X, 4 * X)
        copy = pltpu.make_async_copy(stage.at[rows, :], out.at[rows, :], sem.at[zc])
        copy.start()
        copies.append(copy)
    for copy in copies:
        copy.wait()


def solution(mesh):
    counts = (mesh.shape["gx"], mesh.shape["gy"], mesh.shape["gz"])

    def per_device(potential, charge, permittivity, labels, pattern, blocks):
        Z, X, Y = potential.shape
        A = blocks.shape[-1]
        CZ, CX = Z // 4, X // 4
        NC = CZ * CX
        flat = (Z * X, Y)
        whole = pltpu.VMEM(flat, F32)
        any_spec = pl.BlockSpec(memory_space=pltpu.HBM)
        vmem = pl.BlockSpec(memory_space=pltpu.VMEM)
        n = counts[0]

        swept, spread, cor = pl.pallas_call(
            functools.partial(kernel, counts, Z, X, Y, A),
            out_shape=(whole, pltpu.VMEM((NC, Y), F32), pltpu.VMEM((NC, 128), F32)),
            in_specs=[any_spec] * 6,
            out_specs=(vmem, vmem, vmem),
            scratch_shapes=[
                pltpu.VMEM((CX, 1, 2, CZ), jnp.int32), whole, whole, whole, pltpu.VMEM(flat, jnp.int32), pltpu.VMEM((2 * NC, A, A), F32),
                whole, whole, whole, whole, whole,
                *[pltpu.VMEM((2 * X, Y), F32)] * 2, *[pltpu.VMEM((2 * Z, Y), F32)] * 2, *[pltpu.VMEM((X, 128), F32)] * 2,
                *[pltpu.VMEM((2 * Z, Y), F32)] * 2, pltpu.VMEM((X, 128), F32),
                *[pltpu.VMEM((Z, Y), F32)] * 2,
                pltpu.VMEM((4 * Z, Y), F32), pltpu.VMEM((CZ * X, Y), F32), pltpu.VMEM((CZ * X, Y), F32),
                pltpu.VMEM((CX, CZ * A, 4 * A), BF16), pltpu.VMEM((NC + 2 * CZ, 128), F32), *[pltpu.VMEM((8, 128), F32)] * 3,
                pltpu.VMEM((n * NC, 128), F32), pltpu.VMEM((n * (NC + 2 * CZ), 128), F32), *[pltpu.VMEM((n * 8, 128), F32)] * 4,
                pltpu.VMEM((2 * NC, n * NC), F32),
                pltpu.SemaphoreType.DMA((6,)), pltpu.SemaphoreType.DMA((8,)), pltpu.SemaphoreType.DMA((8,)),
                pltpu.SemaphoreType.DMA((5 * n,)), pltpu.SemaphoreType.DMA((5 * n,)),
            ],
            compiler_params=pltpu.CompilerParams(
                collective_id=0, has_side_effects=True, vmem_limit_bytes=32 * 1024 * 1024),
        )(*[pltpu.with_memory_space_constraint(x, pltpu.HBM) for x in (
            jnp.transpose(pattern, (1, 2, 3, 0)), potential.reshape(flat), charge.reshape(flat), permittivity.reshape(flat),
            labels.reshape(flat), blocks.reshape(2 * NC, A, A))])
        out, corr = pl.pallas_call(
            functools.partial(finish, Z, X, Y, A),
            out_shape=(jax.ShapeDtypeStruct(flat, F32), jax.ShapeDtypeStruct((CZ, CX, 1, A), F32)),
            in_specs=[vmem] * 3,
            out_specs=(any_spec, any_spec),
            scratch_shapes=[whole, pltpu.VMEM((CZ, CX, 1, A), F32), pltpu.SemaphoreType.DMA((CZ + 1,))],
            compiler_params=pltpu.CompilerParams(vmem_limit_bytes=32 * 1024 * 1024),
        )(swept, spread, cor)
        return out.reshape(Z, X, Y), corr

    return jax.shard_map(
        per_device,
        mesh=mesh,
        in_specs=(
            P("gz", "gx", "gy"),
            P("gz", "gx", "gy"),
            P("gz", "gx", "gy"),
            P("gz", "gx", "gy"),
            P("gz", "gx", "gy", None),
            P("gz", "gx", "gy", None, None, None),
        ),
        out_specs=(P("gz", "gx", "gy"), P("gz", "gx", "gy", None)),
        check_vma=False,
    )
```
